32 devices in a mesh: dp: 4 (over y, core), seq: 8 (over z, x).
Axes of the slice: x: 2, y: 2, z: 4, core: 2. Of those that a mesh axis runs over, the one named last changes fastest.
Arguments:
- region: bfloat16 [32, 512, 192], P(('dp', 'seq')), parts along dimension 0, may hold values from -11 to 11
- norm_gain: float32 [192], replicated, may hold values from 0.1 to 1.9
- in_weight: bfloat16 [192, 768], replicated, may hold values from -0.4375 to 0.4375
- conv_weight: float32 [9, 384], replicated, may hold values from -2 to 2
- conv_bias: float32 [384], replicated, may hold values from -3 to 3
- coupling_weight: bfloat16 [384, 512], replicated, may hold values from -0.3125 to 0.3125
- step_weight: bfloat16 [384, 24], replicated, may hold values from -0.3125 to 0.3125
- step_bias: float32 [24], replicated, may hold values from -1 to 1
- decay_log: float32 [24], replicated, may hold values from -16 to -2.9
- skip_gain: float32 [24], replicated, may hold values from 0.5 to 12
- out_gain: float32 [384], replicated, may hold values from 0.1 to 1.9
- out_weight: bfloat16 [384, 192], replicated, may hold values from -0.3125 to 0.3125
Outputs:
- refined: bfloat16 [32, 512, 192], P(('dp', 'seq')), parts along dimension 0
The draws below stay inside these ranges and needn't reach their ends.
There are 4 independent parts, one for each index of `dp`. The reference program is written for one: setup_inputs(seed, part) draws one part's arguments, and reference() takes and returns one part's arrays. A program takes and returns all parts, laid end to end along the dimension named above; an argument that names none is the same for every part. Nothing has to cross between parts.
All inputs are finite; a program needn't handle non-finite values.
Results may differ from the reference program's by a relative error of at most 0.0035.
The reference program's roundings to bfloat16 on the way count: a program that leaves them out, or rounds other values in their place, can miss the bound.
Values may be sent and summed in bfloat16 or wider, within the bound.
A program may use at most 128 MiB of HBM per device.

```python
import math
import jax
import jax.numpy as jnp
from jax import lax

WIDTH = 192
HEADS = 6
STATE = 64
INNER = 384
COLS = 512
BLOCK = 512
ROWS = 8


def draw_decay_log(key, part):
    pick_key, fast_key, middle_key, slow_key = jax.random.split(key, 4)
    entry_count = 4 * HEADS
    quick_share = 0.4
    middle_share = 0.3
    picked = jax.random.uniform(pick_key, (entry_count,))
    fast_rate = jnp.log(jax.random.uniform(fast_key, (entry_count,), minval=1.0 / 50.0, maxval=1.0 / 20.0))
    middle_rate = jax.random.uniform(middle_key, (entry_count,), minval=-6.5, maxval=-5.3)
    slow_rate = jnp.log(jax.random.uniform(slow_key, (entry_count,), minval=0.4, maxval=2.5) / (ROWS * COLS))
    chosen = jnp.where(picked < quick_share, fast_rate, jnp.where(picked < quick_share + middle_share, middle_rate, slow_rate))
    return chosen.astype(jnp.float32)


def draw_region(key, part):
    noise_key, direction_key, level_key, column_key, ramp_key, sign_key, rough_key = jax.random.split(key, 7)
    noise = jnp.clip(jax.random.normal(noise_key, (ROWS, COLS, WIDTH)), -6.0, 6.0)
    direction = jnp.clip(jax.random.normal(direction_key, (WIDTH,)), -3.0, 3.0)
    level = jax.random.uniform(level_key, (ROWS, 1, 1), minval=-1.5, maxval=1.5)
    column_direction = jnp.clip(jax.random.normal(column_key, (WIDTH,)), -3.0, 3.0)
    ramp_size = jax.random.uniform(ramp_key, (), minval=1.2, maxval=2.0)
    ramp_sign = jnp.where(jax.random.uniform(sign_key, ()) < 0.5, -1.0, 1.0)
    places = (2.0 * jnp.arange(COLS, dtype=jnp.float32) + 1.0) / COLS - 1.0
    rough = jnp.repeat(jax.random.uniform(rough_key, (COLS // 16,), minval=-0.5, maxval=0.5), 16)
    column_level = ramp_size * ramp_sign * places + rough
    values = noise + level * direction[None, None, :] + column_level[None, :, None] * column_direction[None, None, :]
    return jnp.clip(values, -11.0, 11.0).astype(jnp.float32).astype(jnp.bfloat16)


def centred(key, extent, scale, bound, kind=jnp.bfloat16):
    return jnp.clip(scale * jax.random.normal(key, extent, jnp.float32), -bound, bound).astype(kind)


def setup_inputs(seed: int = 0, part: int = 0) -> dict:
    key_list = jax.random.split(jax.random.key(seed), 13)
    part_splits = jax.random.split(jax.random.fold_in(key_list[12], part), 13)
    return {
        "region": draw_region(jax.random.fold_in(jax.random.fold_in(key_list[12], part), 71), part),
        "norm_gain": jnp.clip(1.0 + 0.18 * jax.random.normal(key_list[1], (WIDTH,), jnp.float32), 0.1, 1.9),
        "in_weight": centred(key_list[2], (WIDTH, 2 * INNER), WIDTH ** -0.5, 0.4375),
        "conv_weight": centred(key_list[3], (9, INNER), 9 ** -0.5, 2.0, jnp.float32),
        "conv_bias": centred(key_list[4], (INNER,), 0.5, 3.0, jnp.float32),
        "coupling_weight": centred(key_list[5], (INNER, 8 * STATE), INNER ** -0.5, 0.3125),
        "step_weight": centred(key_list[6], (INNER, 4 * HEADS), INNER ** -0.5, 0.3125),
        "step_bias": jnp.clip(jax.random.uniform(key_list[7], (4 * HEADS,), jnp.float32, -1.0, 1.0), -1.0, 1.0),
        "decay_log": draw_decay_log(jax.random.fold_in(key_list[12], 71), part),
        "skip_gain": jnp.clip(jnp.exp(jax.random.uniform(key_list[9], (4 * HEADS,), jnp.float32, math.log(0.5), math.log(12.0))), 0.5, 12.0),
        "out_gain": jnp.clip(1.0 + 0.18 * jax.random.normal(key_list[10], (INNER,), jnp.float32), 0.1, 1.9),
        "out_weight": centred(key_list[11], (INNER, WIDTH), INNER ** -0.5, 0.3125),
    }


EPSILON = 1e-05

def rms_scale(values, gain):
    mean_square = lax.optimization_barrier(jnp.mean(values * values, axis=-1, keepdims=True))
    return values * lax.rsqrt(mean_square + EPSILON) * gain

def block_local(signal, writer, reader, log_decay, step_sizes, skip_part):
    seq_length, inner_width = signal.shape
    head_count = log_decay.shape[1]
    head_size = inner_width // head_count
    block_count = seq_length // BLOCK
    value_blocks = signal.reshape(block_count, BLOCK, head_count, head_size)
    writer_blocks = writer.reshape(block_count, BLOCK, -1)
    reader_blocks = reader.reshape(block_count, BLOCK, -1)
    step_blocks = step_sizes.reshape(block_count, BLOCK, head_count)
    cumul = jnp.cumsum(log_decay.reshape(block_count, BLOCK, head_count), axis=1)
    causal = lax.broadcasted_iota(jnp.int32, (BLOCK, BLOCK), 0) >= lax.broadcasted_iota(jnp.int32, (BLOCK, BLOCK), 1)

    def one_block(pieces):
        value_part, writer_part, reader_part, cumul_part, step_part = pieces
        scores = jnp.dot(reader_part, writer_part.T, preferred_element_type=jnp.float32)
        cum_heads = cumul_part.T
        spread = jnp.where(causal[None], cum_heads[:, :, None] - cum_heads[:, None, :], -jnp.inf)
        mixing = (scores[None] * jnp.exp(spread) * step_part.T[:, None, :]).astype(jnp.bfloat16)
        inside = jnp.einsum('hts,shp->thp', mixing.astype(jnp.float32), value_part.astype(jnp.float32))
        tail_weight = jnp.exp(cumul_part[-1][None, :] - cumul_part) * step_part
        weighted = (value_part * tail_weight[:, :, None]).astype(jnp.bfloat16)
        contrib = jnp.einsum('shp,sn->hpn', weighted.astype(jnp.float32), writer_part.astype(jnp.float32))
        return (inside, contrib)
    inside, contrib = lax.map(one_block, (value_blocks, writer_blocks, reader_blocks, cumul, step_blocks))
    decays = cumul[:, -1, :]

    def advance(carried, pieces):
        decay_now, added = pieces
        return (jnp.exp(decay_now)[:, None, None] * carried + added, carried)
    zero_state = jnp.zeros(contrib.shape[1:], jnp.float32)
    closing, starts = lax.scan(advance, zero_state, (decays, contrib))
    before = jnp.cumsum(decays, axis=0) - decays
    own_part = inside + value_blocks.astype(jnp.float32) * skip_part[None, None, :, None]
    return (own_part, starts, before, cumul, reader_blocks)

def finish(local_terms, carried_in):
    own_part, starts, before, cumul, reader_blocks = local_terms
    entry_state = starts + jnp.exp(before)[:, :, None, None] * carried_in[None]
    entry_half = entry_state.astype(jnp.bfloat16)
    outer_part = jnp.einsum('ktn,khpn->kthp', reader_blocks.astype(jnp.float32), entry_half.astype(jnp.float32))
    result = own_part + outer_part * jnp.exp(cumul)[:, :, :, None]
    return result.reshape(-1, result.shape[2] * result.shape[3])

def column_major(values):
    return jnp.transpose(values, (1, 0, 2)).reshape(values.shape[0] * values.shape[1], values.shape[2])

def reference(region, norm_gain, in_weight, conv_weight, conv_bias, coupling_weight, step_weight, step_bias, decay_log, skip_gain, out_gain, out_weight):
    row_count, col_count, feat_width = region.shape
    inner_width = in_weight.shape[1] // 2
    head_count = step_bias.shape[0] // 4
    head_size = inner_width // head_count
    state_size = coupling_weight.shape[1] // 8
    token_count = row_count * col_count
    flat_region = region.reshape(token_count, feat_width).astype(jnp.float32)
    normed = rms_scale(flat_region, norm_gain).astype(jnp.bfloat16)
    projected = jnp.dot(normed, in_weight, preferred_element_type=jnp.float32).astype(jnp.bfloat16)
    pre_conv = projected[:, :inner_width].reshape(row_count, col_count, inner_width)
    gate_part = projected[:, inner_width:]
    padded = jnp.pad(pre_conv, ((1, 1), (1, 1), (0, 0)))
    summed = conv_bias
    for offset_row in range(3):
        for offset_col in range(3):
            summed = summed + padded[offset_row:offset_row + row_count, offset_col:offset_col + col_count] * conv_weight[offset_row * 3 + offset_col]
    activated = jax.nn.silu(summed).astype(jnp.bfloat16)
    flat_active = activated.reshape(token_count, inner_width)
    coupling = jnp.dot(flat_active, coupling_weight, preferred_element_type=jnp.float32).astype(jnp.bfloat16)
    step_sizes = jax.nn.softplus(jnp.dot(flat_active, step_weight, preferred_element_type=jnp.float32) + step_bias)
    log_decay = -jnp.exp(decay_log) * step_sizes
    outputs = []
    for index in range(4):
        pieces = [flat_active, coupling[:, 2 * index * state_size:(2 * index + 1) * state_size], coupling[:, (2 * index + 1) * state_size:(2 * index + 2) * state_size], log_decay[:, index * head_count:(index + 1) * head_count], step_sizes[:, index * head_count:(index + 1) * head_count]]
        if index >= 2:
            pieces = [column_major(piece.reshape(row_count, col_count, -1)) for piece in pieces]
        if index % 2 == 1:
            pieces = [jnp.flip(piece, 0) for piece in pieces]
        local_terms = block_local(pieces[0], pieces[1], pieces[2], pieces[3], pieces[4], skip_gain[index * head_count:(index + 1) * head_count])
        zero_carry = jnp.zeros((head_count, head_size, state_size), jnp.float32)
        order_out = finish(local_terms, zero_carry)
        if index % 2 == 1:
            order_out = jnp.flip(order_out, 0)
        outputs.append(order_out)
    col_total = (outputs[2] + outputs[3]).astype(jnp.bfloat16)
    col_total = jnp.transpose(col_total.reshape(col_count, row_count, inner_width), (1, 0, 2)).reshape(token_count, inner_width)
    combined = outputs[0] + outputs[1] + col_total.astype(jnp.float32)
    gated = combined * jax.nn.silu(gate_part.astype(jnp.float32))
    normy = rms_scale(gated, out_gain).astype(jnp.bfloat16)
    refined = flat_region + jnp.dot(normy, out_weight, preferred_element_type=jnp.float32)
    return refined.astype(jnp.bfloat16).reshape(row_count, col_count, feat_width)
```

```python
import functools
import math
import jax
import jax.numpy as jnp
from jax import lax
from jax.experimental import pallas as pl
from jax.experimental.pallas import tpu as pltpu
from jax.sharding import PartitionSpec as P

EPSILON = 1e-05
BF = jnp.bfloat16
F32 = jnp.float32
TILE = 128
LOG2E = math.log2(math.e)


def mm(a, b):
    return jnp.dot(a, b, preferred_element_type=F32)


def mm_nt(a, b):
    return lax.dot_general(a, b, (((1,), (1,)), ((), ())), preferred_element_type=F32)


def mm_tn(a, b):
    return lax.dot_general(a, b, (((0,), (0,)), ((), ())), preferred_element_type=F32)


def split(v, count):
    pieces = []
    for _ in range(count):
        piece = v.astype(BF).astype(F32)
        pieces.append(piece)
        v = v - piece
    return jnp.concatenate(pieces, axis=0).astype(BF)


def iota(shape, dim):
    return lax.broadcasted_iota(jnp.int32, shape, dim)


def silu(v):
    return v / (1.0 + jnp.exp(-v))


def bits(v):
    return v.bit_length() - 1


def roll_lanes(v, shift):
    shift = shift % v.shape[1]
    return v if shift == 0 else pltpu.roll(v, shift, 1)


def kernel(
    n,
    heads,
    state,
    block,
    region_hbm,
    norm_gain_ref,
    in_w_hbm,
    conv_w_hbm,
    conv_b_ref,
    coup_w_hbm,
    step_w_hbm,
    step_b_ref,
    decay_ref,
    skip_ref,
    out_gain_ref,
    out_w_hbm,
    out_ref,
    region_ref,
    in_w_ref,
    conv_w_ref,
    coup_w_ref,
    step_w_ref,
    out_w_ref,
    cells,
    got_cells,
    halo,
    pre,
    pcol,
    gate,
    xs,
    coup,
    cum,
    step_t,
    contrib,
    fade,
    grown,
    own,
    msg,
    got,
    tot,
    got_tot,
    ent_out,
    ent_in,
    col_out,
    col_in,
    local_sem,
    r_send,
    r_recv,
    halo_send,
    halo_recv,
    s_send,
    s_recv,
    t_send,
    t_recv,
    e_send,
    e_recv,
    c_send,
    c_recv,
):
    me = lax.axis_index("seq")
    width, tokens = region_ref.shape
    inner = out_w_ref.shape[1]
    band = tokens // n
    head = inner // heads
    part = state // n
    groups = 4 * heads
    count = tokens // block
    span = block // n
    fold = TILE // band
    slab = width // fold
    edge_row = slab

    def peer_of(k):
        return lax.rem(me + k, n)

    def source_of(k):
        return lax.rem(me + n - k, n)

    barrier = pltpu.get_barrier_semaphore()

    def greet(k, _):
        pl.semaphore_signal(barrier, inc=1, device_id={"seq": peer_of(k)})
        return 0

    lax.fori_loop(1, n, greet, 0)

    fetch = [
        pltpu.make_async_copy(source, target, local_sem.at[i])
        for i, (source, target) in enumerate(
            (
                (region_hbm.at[0], region_ref),
                (in_w_hbm, in_w_ref),
                (conv_w_hbm, conv_w_ref),
                (coup_w_hbm, coup_w_ref),
                (step_w_hbm, step_w_ref),
                (out_w_hbm, out_w_ref),
            )
        )
    ]
    for copy in fetch:
        copy.start()

    def r_copy(k, chunk, place):
        return pltpu.make_async_remote_copy(
            src_ref=cells.at[chunk],
            dst_ref=got_cells.at[place],
            send_sem=r_send.at[k],
            recv_sem=r_recv.at[k],
            device_id={"seq": chunk},
        )

    def halo_copy(slot, device):
        return pltpu.make_async_remote_copy(
            src_ref=region_ref,
            dst_ref=halo.at[slot],
            send_sem=halo_send.at[slot],
            recv_sem=halo_recv.at[slot],
            device_id={"seq": device},
        )

    def s_copy(p, k, chunk, place):
        return pltpu.make_async_remote_copy(
            src_ref=msg.at[p, chunk],
            dst_ref=got.at[p, place],
            send_sem=s_send.at[p, k],
            recv_sem=s_recv.at[p, k],
            device_id={"seq": chunk},
        )

    def t_copy(p, k, chunk, place):
        return pltpu.make_async_remote_copy(
            src_ref=tot.at[p],
            dst_ref=got_tot.at[p, place],
            send_sem=t_send.at[p, k],
            recv_sem=t_recv.at[p, k],
            device_id={"seq": chunk},
        )

    def e_copy(p, k, chunk, place):
        return pltpu.make_async_remote_copy(
            src_ref=ent_out.at[p, chunk],
            dst_ref=ent_in.at[p, place],
            send_sem=e_send.at[p, k],
            recv_sem=e_recv.at[p, k],
            device_id={"seq": chunk},
        )

    def c_copy(k, chunk, place):
        return pltpu.make_async_remote_copy(
            src_ref=col_out.at[chunk],
            dst_ref=col_in.at[place],
            send_sem=c_send.at[k],
            recv_sem=c_recv.at[k],
            device_id={"seq": chunk},
        )

    def start_all(make):
        def one(k, _):
            make(k, peer_of(k), me).start()
            return 0

        lax.fori_loop(1, n, one, 0)

    def wait_all(make):
        def one(k, _):
            make(k, peer_of(k), source_of(k)).wait_recv()
            return 0

        lax.fori_loop(1, n, one, 0)

    def wait_sent(make):
        def one(k, _):
            make(k, peer_of(k), source_of(k)).wait_send()
            return 0

        lax.fori_loop(1, n, one, 0)

    piece = jnp.right_shift(iota((slab, TILE), 1), bits(band))
    fetch[0].wait()
    rest = cells.shape[1] - slab - 8
    sel_row = iota((8 * n, tokens), 0)
    sel_band = jnp.right_shift(sel_row, 3)
    sel_kind = jnp.bitwise_and(sel_row, 7)
    sel_cell = iota((8 * n, tokens), 1)
    side = jnp.where(
        jnp.bitwise_and(sel_kind, 1) == 0, sel_band * band - 1, sel_band * band + band
    )
    hit = sel_cell == side
    low = jnp.where(hit & (sel_kind < 2), 1.0, 0.0).astype(BF)
    high = jnp.where(hit & (sel_kind >= 2) & (sel_kind < 4), 1.0, 0.0).astype(BF)
    edges = mm_nt(low, region_ref[0:TILE, :]) + mm_nt(high, region_ref[width - TILE : width, :])
    for m in range(tokens // TILE):
        lanes = region_ref[:, m * TILE : (m + 1) * TILE].astype(F32)
        for r in range(fold):
            packed = lanes[0:slab]
            packed = roll_lanes(packed, (0 - r) * band)
            for q in range(1, fold):
                moved = roll_lanes(lanes[q * slab : (q + 1) * slab], (q - r) * band)
                packed = jnp.where(piece == q, moved, packed)
            d = m * fold + r
            parts = [packed, edges[8 * d : 8 * d + 8]]
            if rest:
                parts.append(jnp.zeros((rest, TILE), F32))
            cells[d] = jnp.concatenate(parts, axis=0).astype(BF)

    pl.semaphore_wait(barrier, n - 1)
    start_all(r_copy)
    got_cells[pl.ds(me, 1)] = cells[pl.ds(me, 1)]

    gain_row = norm_gain_ref[...]
    gain_col = jnp.broadcast_to(gain_row, (8, width)).T[:, 0:1]

    def normed(values):
        mean_square = jnp.mean(values * values, axis=0, keepdims=True)
        return (values * lax.rsqrt(mean_square + EPSILON) * gain_col).astype(BF)

    edge = jnp.zeros((8, inner), F32)
    for a in range(3):
        pre[a, 0:8, :] = edge
        pre[a, tokens + 8 : tokens + 16, :] = edge
    blank = jnp.zeros((band + 16, inner), F32)
    pcol[0] = blank
    pcol[n + 1] = blank
    for i in (1, 2, 5):
        fetch[i].wait()
    mine = mm_tn(normed(region_ref[...].astype(F32)), in_w_ref[...]).astype(BF)
    pre[1, 8 : tokens + 8, :] = mine[:, :inner].astype(F32)
    gate[...] = silu(mine[:, inner:].astype(F32))
    for i in (3, 4):
        fetch[i].wait()

    wait_all(r_copy)

    @pl.when(me < n - 1)
    def _():
        halo_copy(0, me + 1).start()

    @pl.when(me > 0)
    def _():
        halo_copy(1, me - 1).start()

    for m in range(tokens // TILE):
        slabs = []
        for q in range(fold):
            packed = None
            for r in range(fold):
                moved = roll_lanes(
                    got_cells[m * fold + r, 0:slab, :].astype(F32), (r - q) * band
                )
                packed = moved if packed is None else jnp.where(piece == r, moved, packed)
            slabs.append(packed)
        values = normed(jnp.concatenate(slabs, axis=0))
        done = mm_tn(values, in_w_ref[:, :inner]).astype(BF).astype(F32)
        for r in range(fold):
            pcol[m * fold + r + 1, 8 : band + 8, :] = done[r * band : (r + 1) * band]
    rims = jnp.concatenate(
        [got_cells[i, edge_row : cells.shape[1], :].astype(F32)[0:8] for i in range(n)], axis=0
    )
    rim_low = rims
    rim_high = jnp.where(
        iota((8 * n, TILE), 1) >= 2 * TILE - width, pltpu.roll(rims, 8 * n - 2, 0), 0.0
    )
    mean_square = (
        jnp.sum(rim_low * rim_low, axis=-1, keepdims=True)
        + jnp.sum(rim_high * rim_high, axis=-1, keepdims=True)
    ) / width
    scale = lax.rsqrt(mean_square + EPSILON)
    rim_pre = mm(
        (rim_low * scale * gain_row[:, 0:TILE]).astype(BF), in_w_ref[0:TILE, :inner]
    ) + mm(
        (rim_high * scale * gain_row[:, width - TILE : width]).astype(BF),
        in_w_ref[width - TILE : width, :inner],
    )
    rim_pre = rim_pre.astype(BF).astype(F32)
    for i in range(n):
        pcol[i + 1, 7:8, :] = rim_pre[8 * i : 8 * i + 1]
        pcol[i + 1, band + 8 : band + 9, :] = rim_pre[8 * i + 1 : 8 * i + 2]
    for i in range(n):
        summed = conv_b_ref[...]
        for a in range(3):
            for b in range(3):
                tap = 3 * a + b
                summed = summed + pcol[i + a, 7 + b : 7 + b + band, :] * conv_w_ref[tap : tap + 1, :]
        done = silu(summed).astype(BF)
        for c in range(count):
            start = c * block + i * span
            xs[1, start : start + span, :] = done[c * span : (c + 1) * span]

    group = iota((groups, 1), 0)
    behind_group = lax.rem(group, 2 * heads) >= heads
    behind_lane = lax.rem(iota((1, groups), 1), 2 * heads) >= heads
    eye = iota((groups, groups), 0) == iota((groups, groups), 1)

    def column_of(row):
        return jnp.sum(jnp.where(eye, row, 0.0), axis=1, keepdims=True)

    def row_of(column):
        return jnp.sum(jnp.where(eye, column, 0.0), axis=0, keepdims=True)

    rates = -jnp.exp(column_of(decay_ref[...]))
    step_b = column_of(step_b_ref[...])
    skips = column_of(skip_ref[...])

    def spreader(p):
        where = jnp.right_shift(iota((groups, 2 * inner), 1), bits(head))
        return (iota((groups, 2 * inner), 0) == where + p * 2 * heads).astype(F32)

    def spread(v, e, pieces):
        many = jnp.concatenate([e] * pieces, axis=0).astype(BF)
        return mm_tn(split(v, pieces), many)

    def position(p, v):
        if p == 0:
            return v
        return jnp.bitwise_and(v, span - 1) * n + jnp.right_shift(v, bits(span))

    def rows_of(c):
        return slice(c * block, (c + 1) * block)

    def prepare(p):
        x = xs[p]
        first = p * 4 * state
        coup[p] = mm(x, coup_w_ref[:, first : first + 4 * state]).astype(BF)
        logits = mm_nt(step_w_ref[...], x) + step_b
        steps = jnp.maximum(logits, 0.0) + jnp.log1p(jnp.exp(-jnp.abs(logits)))
        logs = rates * steps
        step_t[p] = steps
        pieces = split(logs, 3)
        earlier = position(p, iota((block, block), 0)) <= position(p, iota((block, block), 1))
        earlier = jnp.where(earlier, 1.0, 0.0).astype(BF)
        e = spreader(p)
        lane = iota((groups, TILE), 1)
        totals = jnp.zeros((groups, TILE), F32)
        whole = jnp.zeros((groups, 1), F32)
        for c in range(count):
            rows = rows_of(c)
            sums = mm(pieces[:, rows], earlier)
            ahead = sums[0:groups] + sums[groups : 2 * groups] + sums[2 * groups : 3 * groups]
            total = ahead[:, block - 1 : block]
            level = jnp.where(behind_group, total - ahead + logs[:, rows], ahead)
            cum[p, :, rows] = level
            totals = jnp.where(lane == c, total, totals)
            whole = whole + total
            tails = spread(jnp.exp(total - level) * steps[:, rows], e, 2)
            xf = xs[p, rows, :].astype(F32)
            for o in range(2):
                weighted = (xf * tails[:, o * inner : (o + 1) * inner]).astype(BF)
                writer = coup[p, rows, 2 * o * state : (2 * o + 1) * state]
                contrib[p, o, c] = mm_tn(writer, weighted)
        tot[p, :, 0:groups] = jnp.broadcast_to(row_of(whole), (8, groups))
        start_all(functools.partial(t_copy, p))
        got_tot[p, pl.ds(me, 1)] = tot[p][None]
        fade[p] = spread(jnp.exp(totals), e, 3)[0:8]
        sums = [contrib[p, 0, 0], contrib[p, 1, count - 1]]
        for c in range(1, count):
            sums[0] = fade[p, c : c + 1, :inner] * sums[0] + contrib[p, 0, c]
            back = count - 1 - c
            sums[1] = fade[p, back : back + 1, inner:] * sums[1] + contrib[p, 1, back]
        for d in range(n):
            pieces = [v[d * part : (d + 1) * part] for v in sums]
            if 2 * part < 16:
                pieces.append(jnp.zeros((16 - 2 * part, inner), F32))
            msg[p, d] = jnp.concatenate(pieces, axis=0).astype(BF)
        start_all(functools.partial(s_copy, p))
        got[p, pl.ds(me, 1)] = msg[p, pl.ds(me, 1)]

    def local(p):
        e = spreader(p)
        both_sides = e[:, :inner] + e[:, inner:]
        eyes = eye.astype(F32)
        rows_tile = min(block, TILE)
        even = jnp.bitwise_and(iota((1, 2 * head), 1), head) == 0
        for c in range(count):
            rows = rows_of(c)
            level = cum[p, :, rows]
            steps = step_t[p, :, rows]
            grown[p, rows, :] = spread(jnp.exp(level), e, 2)
            scaled = level * LOG2E
            source = scaled - jnp.log(steps) * LOG2E
            target = spread(scaled, eyes, 3)
            xf = xs[p, rows, :].astype(F32)
            pairs = []
            for j in range(heads // 2):
                lanes = xf[:, 2 * j * head : 2 * (j + 1) * head]
                pairs.append(
                    jnp.concatenate(
                        [jnp.where(even, lanes, 0.0), jnp.where(even, 0.0, lanes)], axis=0
                    ).astype(BF)
                )
            diagonals = [jnp.zeros((1, block), F32)] * 2
            for q in range(block // rows_tile):
                t0 = q * rows_tile
                mine = coup[p, c * block + t0 : c * block + t0 + rows_tile, :]
                ahead = mm_nt(mine[:, state : 2 * state], coup[p, rows, 0:state])
                behind = mm_nt(mine[:, 3 * state :], coup[p, rows, 2 * state : 3 * state])
                t = iota((rows_tile, block), 0) + t0
                s = iota((rows_tile, block), 1)
                after = position(p, t) > position(p, s)
                same = t == s
                scores = jnp.where(same, 0.0, jnp.where(after, ahead, behind))
                for o, v in enumerate((ahead, behind)):
                    found = jnp.sum(jnp.where(same, v, 0.0), axis=0, keepdims=True)
                    diagonals[o] = diagonals[o] + found

                def weights(h):
                    f = p * 2 * heads + h
                    g = f + heads
                    lead = target[t0 : t0 + rows_tile, f : f + 1] - source[f : f + 1, :]
                    back = target[t0 : t0 + rows_tile, g : g + 1] - source[g : g + 1, :]
                    return (scores * jnp.exp2(jnp.where(after, lead, back))).astype(BF)

                for j in range(heads // 2):
                    pair = jnp.concatenate([weights(2 * j), weights(2 * j + 1)], axis=1)
                    own[
                        p,
                        c * block + t0 : c * block + t0 + rows_tile,
                        2 * j * head : 2 * (j + 1) * head,
                    ] = mm(pair, pairs[j])
            diag = jnp.where(behind_group, diagonals[1], diagonals[0]) * steps
            diag = diag.astype(BF).astype(F32) + skips
            own[p, rows, :] += xf * spread(diag, both_sides, 2)

    def scan(p):
        wait_all(functools.partial(t_copy, p))
        e = spreader(p)
        logs = jnp.concatenate([got_tot[p, i, :, 0:groups] for i in range(n)], axis=0)
        pieces = split(jnp.exp(logs), 3).reshape(3, 8 * n, groups)
        fades = sum(mm(pieces[i], e.astype(BF)) for i in range(3))
        wait_all(functools.partial(s_copy, p))
        entry = jnp.zeros((part, inner), F32)
        ahead = []
        for i in range(n):
            ahead.append(entry)
            entry = fades[8 * i : 8 * i + 1, :inner] * entry + got[p, i].astype(F32)[0:part]
        entry = jnp.zeros((part, inner), F32)
        for i in reversed(range(n)):
            pieces = [ahead[i], entry]
            if 2 * part < 16:
                pieces.append(jnp.zeros((16 - 2 * part, inner), F32))
            ent_out[p, i] = jnp.concatenate(pieces, axis=0).astype(BF)
            entry = (
                fades[8 * i : 8 * i + 1, inner:] * entry + got[p, i].astype(F32)[part : 2 * part]
            )
        start_all(functools.partial(e_copy, p))
        ent_in[p, pl.ds(me, 1)] = ent_out[p, pl.ds(me, 1)]

    def finish(p):
        wait_all(functools.partial(e_copy, p))
        arrived = [ent_in[p, i].astype(F32) for i in range(n)]
        entries = [[None] * count, [None] * count]
        for o in range(2):
            entry = jnp.concatenate([v[o * part : (o + 1) * part] for v in arrived], axis=0)
            order = range(count) if o == 0 else reversed(range(count))
            for c in order:
                entries[o][c] = entry.astype(BF)
                lanes = slice(o * inner, (o + 1) * inner)
                entry = fade[p, c : c + 1, lanes] * entry + contrib[p, o, c]
        for c in range(count):
            rows = rows_of(c)
            result = own[p, rows, :]
            for o in range(2):
                reader = coup[p, rows, (2 * o + 1) * state : (2 * o + 2) * state]
                carried = mm(reader, entries[o][c])
                result = result + carried * grown[p, rows, o * inner : (o + 1) * inner]
            if p == 0:
                own[p, rows, :] = result
            else:
                result = result.astype(BF)
                for i in range(n):
                    col_out[i, c * span : (c + 1) * span, :] = result[i * span : (i + 1) * span]

    prepare(1)
    local(1)
    scan(1)

    @pl.when(me < n - 1)
    def _():
        halo_copy(1, me + 1).wait_recv()
        halo_copy(0, me + 1).wait_send()

    @pl.when(me == n - 1)
    def _():
        halo[1] = jnp.zeros((width, tokens), BF)

    @pl.when(me > 0)
    def _():
        halo_copy(0, me - 1).wait_recv()
        halo_copy(1, me - 1).wait_send()

    @pl.when(me == 0)
    def _():
        halo[0] = jnp.zeros((width, tokens), BF)

    for slot, a in ((0, 0), (1, 2)):
        rim = mm_tn(normed(halo[slot].astype(F32)), in_w_ref[:, :inner]).astype(BF)
        pre[a, 8 : tokens + 8, :] = rim.astype(F32)
    for c in range(tokens // TILE):
        summed = conv_b_ref[...]
        for a in range(3):
            for b in range(3):
                first = c * TILE + 7 + b
                tap = 3 * a + b
                summed = summed + pre[a, first : first + TILE, :] * conv_w_ref[tap : tap + 1, :]
        xs[0, c * TILE : (c + 1) * TILE, :] = silu(summed).astype(BF)
    prepare(0)
    finish(1)
    start_all(c_copy)
    col_in[pl.ds(me, 1)] = col_out[pl.ds(me, 1)]
    local(0)
    scan(0)
    finish(0)
    wait_all(c_copy)
    for c in range(tokens // TILE):
        rows = slice(c * TILE, (c + 1) * TILE)
        per = TILE // band
        col = col_in[c * per : (c + 1) * per].astype(F32).reshape(TILE, inner)
        gated = (own[0, rows, :] + col) * gate[rows, :]
        mean_square = jnp.mean(gated * gated, axis=-1, keepdims=True)
        normy = (gated * lax.rsqrt(mean_square + EPSILON) * out_gain_ref[...]).astype(BF)
        out_ref[0, :, rows] = (
            region_ref[:, rows].astype(F32) + mm_nt(out_w_ref[...], normy)
        ).astype(BF)
    wait_sent(r_copy)
    for p in range(2):
        wait_sent(functools.partial(s_copy, p))
        wait_sent(functools.partial(t_copy, p))
        wait_sent(functools.partial(e_copy, p))
    wait_sent(c_copy)


def body(n, *args):
    region = args[0]
    _, tokens, width = region.shape
    inner = args[11].shape[0]
    groups = args[7].shape[0]
    heads = groups // 4
    state = args[5].shape[1] // 8
    band = tokens // n
    part = state // n
    block = max(TILE, 16 * n)
    count = tokens // block
    fold = TILE // band
    cell_rows = (width // fold + 8 + 15) // 16 * 16
    flat = [v if v.ndim > 1 else v.reshape(1, -1) for v in args]
    flat[0] = jnp.swapaxes(region, 1, 2)
    flat[6] = flat[6].T
    flat[11] = flat[11].T
    ent_rows = max(16, 2 * part)
    dma = pltpu.SemaphoreType.DMA
    vmem = pltpu.VMEM
    in_hbm = (0, 2, 3, 5, 6, 11)
    out = pl.pallas_call(
        functools.partial(kernel, n, heads, state, block),
        out_shape=jax.ShapeDtypeStruct(flat[0].shape, BF),
        in_specs=[
            pl.BlockSpec(memory_space=pl.ANY if i in in_hbm else pltpu.VMEM)
            for i in range(len(flat))
        ],
        out_specs=pl.BlockSpec(memory_space=pltpu.VMEM),
        scratch_shapes=[
            vmem((width, tokens), BF),
            *[vmem(flat[i].shape, flat[i].dtype) for i in in_hbm[1:]],
            vmem((n, cell_rows, TILE), BF),
            vmem((n, cell_rows, TILE), BF),
            vmem((2, width, tokens), BF),
            vmem((3, tokens + 16, inner), F32),
            vmem((n + 2, band + 16, inner), F32),
            vmem((tokens, inner), F32),
            vmem((2, tokens, inner), BF),
            vmem((2, tokens, 4 * state), BF),
            vmem((2, groups, tokens), F32),
            vmem((2, groups, tokens), F32),
            vmem((2, 2, count, state, inner), F32),
            vmem((2, 8, 2 * inner), F32),
            vmem((2, tokens, 2 * inner), F32),
            vmem((2, tokens, inner), F32),
            vmem((2, n, ent_rows, inner), BF),
            vmem((2, n, ent_rows, inner), BF),
            vmem((2, 8, 128), F32),
            vmem((2, n, 8, 128), F32),
            vmem((2, n, ent_rows, inner), BF),
            vmem((2, n, ent_rows, inner), BF),
            vmem((n, band, inner), BF),
            vmem((n, band, inner), BF),
            dma((6,)),
            dma((n,)),
            dma((n,)),
            dma((2,)),
            dma((2,)),
            dma((2, n)),
            dma((2, n)),
            dma((2, n)),
            dma((2, n)),
            dma((2, n)),
            dma((2, n)),
            dma((n,)),
            dma((n,)),
        ],
        compiler_params=pltpu.CompilerParams(
            collective_id=0, has_side_effects=True, vmem_limit_bytes=56 * 1024 * 1024
        ),
    )(*flat)
    return jnp.swapaxes(out, 1, 2)


def solution(mesh):
    in_specs = (P(("dp", "seq"), None, None),) + (P(),) * 11
    return jax.shard_map(
        functools.partial(body, mesh.shape["seq"]),
        mesh=mesh,
        in_specs=in_specs,
        out_specs=P(("dp", "seq"), None, None),
        check_vma=False,
    )
```

```python
import functools
import math
import jax
import jax.numpy as jnp
from jax import lax
from jax.experimental import pallas as pl
from jax.experimental.pallas import tpu as pltpu
from jax.sharding import PartitionSpec as P

EPSILON = 1e-05
BF = jnp.bfloat16
F32 = jnp.float32
TILE = 128
LOG2E = math.log2(math.e)


def mm(a, b):
    return jnp.dot(a, b, preferred_element_type=F32)


def mm_nt(a, b):
    return lax.dot_general(a, b, (((1,), (1,)), ((), ())), preferred_element_type=F32)


def mm_tn(a, b):
    return lax.dot_general(a, b, (((0,), (0,)), ((), ())), preferred_element_type=F32)


def split(v, count):
    pieces = []
    for _ in range(count):
        piece = v.astype(BF).astype(F32)
        pieces.append(piece)
        v = v - piece
    return jnp.concatenate(pieces, axis=0).astype(BF)


def iota(shape, dim):
    return lax.broadcasted_iota(jnp.int32, shape, dim)


def silu(v):
    half = 0.5 * v
    return half * jnp.tanh(half) + half


def depthwise(planes, weights, bias, size):
    sums = []
    for b in range(3):
        total = planes[0] * weights[b : b + 1, :]
        for a in (1, 2):
            tap = 3 * a + b
            total = total + planes[a] * weights[tap : tap + 1, :]
        sums.append(total)
    rows = sums[0].shape[0]
    moved = pltpu.roll(sums[0], 1, 0) + pltpu.roll(sums[2], rows - 1, 0)
    return silu((sums[1] + moved)[8 : 8 + size] + bias)


def bits(v):
    return v.bit_length() - 1


def one_row(ref):
    return jnp.concatenate([ref[i : i + 1, :] for i in range(ref.shape[0])], axis=1)


def roll_lanes(v, shift):
    shift = shift % v.shape[1]
    return v if shift == 0 else pltpu.roll(v, shift, 1)


def kernel(
    n,
    heads,
    state,
    block,
    region_hbm,
    norm_gain_ref,
    in_w_hbm,
    conv_w_hbm,
    conv_b_ref,
    coup_w_hbm,
    step_w_hbm,
    step_b_ref,
    decay_ref,
    skip_ref,
    out_gain_ref,
    out_w_hbm,
    out_ref,
    region_ref,
    in_w_ref,
    conv_w_ref,
    coup_w_ref,
    step_w_ref,
    out_w_ref,
    cells,
    got_cells,
    halo,
    pre,
    pcol,
    gate,
    xs,
    coup,
    cum,
    step_t,
    contrib,
    fade,
    grown,
    own,
    msg,
    got,
    ent_out,
    ent_in,
    col_out,
    col_in,
    local_sem,
    r_send,
    r_recv,
    halo_send,
    halo_recv,
    s_send,
    s_recv,
    e_send,
    e_recv,
    c_send,
    c_recv,
):
    me = lax.axis_index("seq")
    width, tokens = region_ref.shape
    inner = out_w_ref.shape[1]
    band = tokens // n
    head = inner // heads
    part = state // n
    groups = 4 * heads
    count = tokens // block
    span = block // n
    fold = TILE // band
    slab = width // fold
    edge_row = slab

    def peer_of(k):
        return lax.rem(me + k, n)

    def source_of(k):
        return lax.rem(me + n - k, n)

    barrier = pltpu.get_barrier_semaphore()

    def greet(k, _):
        pl.semaphore_signal(barrier, inc=1, device_id={"seq": peer_of(k)})
        return 0

    lax.fori_loop(1, n, greet, 0)

    fetch = [
        pltpu.make_async_copy(source, target, local_sem.at[i])
        for i, (source, target) in enumerate(
            (
                (region_hbm.at[0], region_ref),
                (in_w_hbm, in_w_ref),
                (conv_w_hbm, conv_w_ref),
                (coup_w_hbm, coup_w_ref),
                (step_w_hbm, step_w_ref),
                (out_w_hbm, out_w_ref),
            )
        )
    ]
    for copy in fetch:
        copy.start()

    def r_copy(k, chunk, place):
        return pltpu.make_async_remote_copy(
            src_ref=cells.at[chunk],
            dst_ref=got_cells.at[place],
            send_sem=r_send.at[k],
            recv_sem=r_recv.at[k],
            device_id={"seq": chunk},
        )

    def halo_copy(slot, device):
        return pltpu.make_async_remote_copy(
            src_ref=region_ref,
            dst_ref=halo.at[slot],
            send_sem=halo_send.at[slot],
            recv_sem=halo_recv.at[slot],
            device_id={"seq": device},
        )

    def s_copy(p, k, chunk, place):
        return pltpu.make_async_remote_copy(
            src_ref=msg.at[p, chunk],
            dst_ref=got.at[p, place],
            send_sem=s_send.at[p, k],
            recv_sem=s_recv.at[p, k],
            device_id={"seq": chunk},
        )

    def e_copy(p, k, chunk, place):
        return pltpu.make_async_remote_copy(
            src_ref=ent_out.at[p, chunk],
            dst_ref=ent_in.at[p, place],
            send_sem=e_send.at[p, k],
            recv_sem=e_recv.at[p, k],
            device_id={"seq": chunk},
        )

    def c_copy(k, chunk, place):
        return pltpu.make_async_remote_copy(
            src_ref=col_out.at[chunk],
            dst_ref=col_in.at[place],
            send_sem=c_send.at[k],
            recv_sem=c_recv.at[k],
            device_id={"seq": chunk},
        )

    def start_all(make):
        def one(k, _):
            make(k, peer_of(k), me).start()
            return 0

        lax.fori_loop(1, n, one, 0)

    def wait_all(make):
        def one(k, _):
            make(k, peer_of(k), source_of(k)).wait_recv()
            return 0

        lax.fori_loop(1, n, one, 0)

    def wait_sent(make):
        def one(k, _):
            make(k, peer_of(k), source_of(k)).wait_send()
            return 0

        lax.fori_loop(1, n, one, 0)

    piece = jnp.right_shift(iota((slab, TILE), 1), bits(band))
    fetch[0].wait()
    rest = cells.shape[1] - slab - 8
    sel_row = iota((8 * n, tokens), 0)
    sel_band = jnp.right_shift(sel_row, 3)
    sel_kind = jnp.bitwise_and(sel_row, 7)
    sel_cell = iota((8 * n, tokens), 1)
    side = jnp.where(
        jnp.bitwise_and(sel_kind, 1) == 0, sel_band * band - 1, sel_band * band + band
    )
    hit = sel_cell == side
    low = jnp.where(hit & (sel_kind < 2), 1.0, 0.0).astype(BF)
    high = jnp.where(hit & (sel_kind >= 2) & (sel_kind < 4), 1.0, 0.0).astype(BF)
    edges = mm_nt(low, region_ref[0:TILE, :]) + mm_nt(high, region_ref[width - TILE : width, :])
    for m in range(tokens // TILE):
        lanes = region_ref[:, m * TILE : (m + 1) * TILE].astype(F32)
        for r in range(fold):
            packed = lanes[0:slab]
            packed = roll_lanes(packed, (0 - r) * band)
            for q in range(1, fold):
                moved = roll_lanes(lanes[q * slab : (q + 1) * slab], (q - r) * band)
                packed = jnp.where(piece == q, moved, packed)
            d = m * fold + r
            parts = [packed, edges[8 * d : 8 * d + 8]]
            if rest:
                parts.append(jnp.zeros((rest, TILE), F32))
            cells[d] = jnp.concatenate(parts, axis=0).astype(BF)

    pl.semaphore_wait(barrier, n - 1)
    start_all(r_copy)

    @pl.when(me < n - 1)
    def _():
        halo_copy(0, me + 1).start()

    @pl.when(me > 0)
    def _():
        halo_copy(1, me - 1).start()

    got_cells[pl.ds(me, 1)] = cells[pl.ds(me, 1)]

    gain_row = norm_gain_ref[...]
    conv_b = one_row(conv_b_ref)
    out_gain = one_row(out_gain_ref)
    gain_col = jnp.broadcast_to(gain_row, (8, width)).T[:, 0:1]

    def normed(values):
        mean_square = jnp.mean(values * values, axis=0, keepdims=True)
        return (values * lax.rsqrt(mean_square + EPSILON) * gain_col).astype(BF)

    edge = jnp.zeros((8, inner), F32)
    for a in range(3):
        pre[a, 0:8, :] = edge
        pre[a, tokens + 8 : tokens + 16, :] = edge
    blank = jnp.zeros((band + 16, inner), F32)
    pcol[0] = blank
    pcol[n + 1] = blank
    for i in (1, 2, 5):
        fetch[i].wait()
    mine = mm_tn(normed(region_ref[...].astype(F32)), in_w_ref[...]).astype(BF)
    pre[1, 8 : tokens + 8, :] = mine[:, :inner].astype(F32)
    gate[...] = silu(mine[:, inner:].astype(F32))
    for i in (3, 4):
        fetch[i].wait()

    wait_all(r_copy)

    for m in range(tokens // TILE):
        slabs = []
        for q in range(fold):
            packed = None
            for r in range(fold):
                moved = roll_lanes(
                    got_cells[m * fold + r, 0:slab, :].astype(F32), (r - q) * band
                )
                packed = moved if packed is None else jnp.where(piece == r, moved, packed)
            slabs.append(packed)
        values = normed(jnp.concatenate(slabs, axis=0))
        done = mm_tn(values, in_w_ref[:, :inner]).astype(BF).astype(F32)
        for r in range(fold):
            pcol[m * fold + r + 1, 8 : band + 8, :] = done[r * band : (r + 1) * band]
    rims = jnp.concatenate(
        [got_cells[i, edge_row : cells.shape[1], :].astype(F32)[0:8] for i in range(n)], axis=0
    )
    rim_low = rims
    rim_high = jnp.where(
        iota((8 * n, TILE), 1) >= 2 * TILE - width, pltpu.roll(rims, 8 * n - 2, 0), 0.0
    )
    mean_square = (
        jnp.sum(rim_low * rim_low, axis=-1, keepdims=True)
        + jnp.sum(rim_high * rim_high, axis=-1, keepdims=True)
    ) / width
    scale = lax.rsqrt(mean_square + EPSILON)
    rim_pre = mm(
        (rim_low * scale * gain_row[:, 0:TILE]).astype(BF), in_w_ref[0:TILE, :inner]
    ) + mm(
        (rim_high * scale * gain_row[:, width - TILE : width]).astype(BF),
        in_w_ref[width - TILE : width, :inner],
    )
    rim_pre = rim_pre.astype(BF).astype(F32)
    for i in range(n):
        pcol[i + 1, 7:8, :] = rim_pre[8 * i : 8 * i + 1]
        pcol[i + 1, band + 8 : band + 9, :] = rim_pre[8 * i + 1 : 8 * i + 2]
    for i in range(n):
        planes = [pcol[i + a] for a in range(3)]
        done = depthwise(planes, conv_w_ref, conv_b, band).astype(BF)
        for c in range(count):
            start = c * block + i * span
            xs[1, start : start + span, :] = done[c * span : (c + 1) * span]

    group = iota((groups, 1), 0)
    behind_group = lax.rem(group, 2 * heads) >= heads
    behind_lane = lax.rem(iota((1, groups), 1), 2 * heads) >= heads
    eye = iota((groups, groups), 0) == iota((groups, groups), 1)

    def column_of(row):
        return jnp.sum(jnp.where(eye, row, 0.0), axis=1, keepdims=True)

    def row_of(column):
        here = iota((groups, TILE), 0) == iota((groups, TILE), 1)
        return jnp.sum(jnp.where(here, column, 0.0), axis=0, keepdims=True)

    rates = -jnp.exp(column_of(decay_ref[...]))
    step_b = column_of(step_b_ref[...])
    skips = column_of(skip_ref[...])

    def spreader(p):
        where = jnp.right_shift(iota((groups, 2 * inner), 1), bits(head))
        return (iota((groups, 2 * inner), 0) == where + p * 2 * heads).astype(F32)

    def spread(v, e, pieces):
        many = jnp.concatenate([e] * pieces, axis=0).astype(BF)
        return mm_tn(split(v, pieces), many)

    def position(p, v):
        if p == 0:
            return v
        return jnp.bitwise_and(v, span - 1) * n + jnp.right_shift(v, bits(span))

    def rows_of(c):
        return slice(c * block, (c + 1) * block)

    def prepare(p):
        x = xs[p]
        first = p * 4 * state
        coup[p] = mm(x, coup_w_ref[:, first : first + 4 * state]).astype(BF)
        logits = mm_nt(step_w_ref[...], x) + step_b
        steps = jnp.maximum(logits, 0.0) + jnp.log1p(jnp.exp(-jnp.abs(logits)))
        logs = rates * steps
        step_t[p] = steps
        pieces = split(logs, 3)
        earlier = position(p, iota((block, block), 0)) <= position(p, iota((block, block), 1))
        earlier = jnp.where(earlier, 1.0, 0.0).astype(BF)
        e = spreader(p)
        lane = iota((groups, TILE), 1)
        totals = jnp.zeros((groups, TILE), F32)
        whole = jnp.zeros((groups, 1), F32)
        for c in range(count):
            rows = rows_of(c)
            sums = mm(pieces[:, rows], earlier)
            ahead = sums[0:groups] + sums[groups : 2 * groups] + sums[2 * groups : 3 * groups]
            total = ahead[:, block - 1 : block]
            level = jnp.where(behind_group, total - ahead + logs[:, rows], ahead)
            cum[p, :, rows] = level
            totals = jnp.where(lane == c, total, totals)
            whole = whole + total
            tails = spread(jnp.exp(total - level) * steps[:, rows], e, 2)
            xf = xs[p, rows, :].astype(F32)
            for o in range(2):
                weighted = (xf * tails[:, o * inner : (o + 1) * inner]).astype(BF)
                writer = coup[p, rows, 2 * o * state : (2 * o + 1) * state]
                contrib[p, o, c] = mm_tn(writer, weighted)
        left = row_of(whole)
        line = iota((msg.shape[2], TILE), 0)
        totals_sent = jnp.zeros((msg.shape[2], TILE), F32)
        for i in range(3):
            rounded = left.astype(BF).astype(F32)
            totals_sent = jnp.where(line == i, rounded, totals_sent)
            left = left - rounded
        totals_sent = totals_sent.astype(BF)
        fade[p] = spread(jnp.exp(totals), e, 3)[0:8]
        sums = [contrib[p, 0, 0], contrib[p, 1, count - 1]]
        for c in range(1, count):
            sums[0] = fade[p, c : c + 1, :inner] * sums[0] + contrib[p, 0, c]
            back = count - 1 - c
            sums[1] = fade[p, back : back + 1, inner:] * sums[1] + contrib[p, 1, back]
        for d in range(n):
            pieces = [v[d * part : (d + 1) * part] for v in sums]
            if 2 * part < 16:
                pieces.append(jnp.zeros((16 - 2 * part, inner), F32))
            msg[p, d, :, 0:inner] = jnp.concatenate(pieces, axis=0).astype(BF)
            msg[p, d, :, inner:] = totals_sent
        start_all(functools.partial(s_copy, p))
        got[p, pl.ds(me, 1)] = msg[p, pl.ds(me, 1)]

    def local(p):
        e = spreader(p)
        both_sides = e[:, :inner] + e[:, inner:]
        eyes = eye.astype(F32)
        rows_tile = min(block, TILE)
        even = jnp.bitwise_and(iota((1, 2 * head), 1), head) == 0
        for c in range(count):
            rows = rows_of(c)
            level = cum[p, :, rows]
            steps = step_t[p, :, rows]
            grown[p, rows, :] = spread(jnp.exp(level), e, 2)
            scaled = level * LOG2E
            source = scaled - jnp.log(steps) * LOG2E
            target = spread(scaled, eyes, 3)
            xf = xs[p, rows, :].astype(F32)
            pairs = []
            for j in range(heads // 2):
                lanes = xf[:, 2 * j * head : 2 * (j + 1) * head]
                pairs.append(
                    jnp.concatenate(
                        [jnp.where(even, lanes, 0.0), jnp.where(even, 0.0, lanes)], axis=0
                    ).astype(BF)
                )
            diagonals = [jnp.zeros((1, block), F32)] * 2
            for q in range(block // rows_tile):
                t0 = q * rows_tile
                mine = coup[p, c * block + t0 : c * block + t0 + rows_tile, :]
                ahead = mm_nt(mine[:, state : 2 * state], coup[p, rows, 0:state])
                behind = mm_nt(mine[:, 3 * state :], coup[p, rows, 2 * state : 3 * state])
                t = iota((rows_tile, block), 0) + t0
                s = iota((rows_tile, block), 1)
                after = position(p, t) > position(p, s)
                same = t == s
                scores = jnp.where(same, 0.0, jnp.where(after, ahead, behind))
                for o, v in enumerate((ahead, behind)):
                    found = jnp.sum(jnp.where(same, v, 0.0), axis=0, keepdims=True)
                    diagonals[o] = diagonals[o] + found

                def weights(h):
                    f = p * 2 * heads + h
                    g = f + heads
                    lead = target[t0 : t0 + rows_tile, f : f + 1] - source[f : f + 1, :]
                    back = target[t0 : t0 + rows_tile, g : g + 1] - source[g : g + 1, :]
                    return (scores * jnp.exp2(jnp.where(after, lead, back))).astype(BF)

                for j in range(heads // 2):
                    pair = jnp.concatenate([weights(2 * j), weights(2 * j + 1)], axis=1)
                    own[
                        p,
                        c * block + t0 : c * block + t0 + rows_tile,
                        2 * j * head : 2 * (j + 1) * head,
                    ] = mm(pair, pairs[j])
            diag = jnp.where(behind_group, diagonals[1], diagonals[0]) * steps
            diag = diag.astype(BF).astype(F32) + skips
            own[p, rows, :] += xf * spread(diag, both_sides, 2)

    def scan(p):
        wait_all(functools.partial(s_copy, p))
        e = spreader(p)
        logs = jnp.concatenate(
            [got[p, i, :, inner:].astype(F32)[0:8] for i in range(n)], axis=0
        )
        logs = logs + pltpu.roll(logs, 8 * n - 1, 0) + pltpu.roll(logs, 8 * n - 2, 0)
        pieces = split(jnp.exp(logs[:, 0:groups]), 3).reshape(3, 8 * n, groups)
        fades = sum(mm(pieces[i], e.astype(BF)) for i in range(3))
        entry = jnp.zeros((part, inner), F32)
        ahead = []
        for i in range(n):
            ahead.append(entry)
            entry = fades[8 * i : 8 * i + 1, :inner] * entry + got[p, i, :, 0:inner].astype(F32)[0:part]
        entry = jnp.zeros((part, inner), F32)
        for i in reversed(range(n)):
            pieces = [ahead[i], entry]
            if 2 * part < 16:
                pieces.append(jnp.zeros((16 - 2 * part, inner), F32))
            ent_out[p, i] = jnp.concatenate(pieces, axis=0).astype(BF)
            entry = (
                fades[8 * i : 8 * i + 1, inner:] * entry + got[p, i, :, 0:inner].astype(F32)[part : 2 * part]
            )
        start_all(functools.partial(e_copy, p))
        ent_in[p, pl.ds(me, 1)] = ent_out[p, pl.ds(me, 1)]

    def finish(p):
        wait_all(functools.partial(e_copy, p))
        arrived = [ent_in[p, i].astype(F32) for i in range(n)]
        entries = [[None] * count, [None] * count]
        for o in range(2):
            entry = jnp.concatenate([v[o * part : (o + 1) * part] for v in arrived], axis=0)
            order = range(count) if o == 0 else reversed(range(count))
            for c in order:
                entries[o][c] = entry.astype(BF)
                lanes = slice(o * inner, (o + 1) * inner)
                entry = fade[p, c : c + 1, lanes] * entry + contrib[p, o, c]
        for c in range(count):
            rows = rows_of(c)
            result = own[p, rows, :]
            for o in range(2):
                reader = coup[p, rows, (2 * o + 1) * state : (2 * o + 2) * state]
                carried = mm(reader, entries[o][c])
                result = result + carried * grown[p, rows, o * inner : (o + 1) * inner]
            if p == 0:
                own[p, rows, :] = result
            else:
                result = result.astype(BF)
                for i in range(n):
                    col_out[i, c * span : (c + 1) * span, :] = result[i * span : (i + 1) * span]

    prepare(1)
    @pl.when(me < n - 1)
    def _():
        halo_copy(1, me + 1).wait_recv()
        halo_copy(0, me + 1).wait_send()

    @pl.when(me == n - 1)
    def _():
        halo[1] = jnp.zeros((width, tokens), BF)

    @pl.when(me > 0)
    def _():
        halo_copy(0, me - 1).wait_recv()
        halo_copy(1, me - 1).wait_send()

    @pl.when(me == 0)
    def _():
        halo[0] = jnp.zeros((width, tokens), BF)

    for slot, a in ((0, 0), (1, 2)):
        rim = mm_tn(normed(halo[slot].astype(F32)), in_w_ref[:, :inner]).astype(BF)
        pre[a, 8 : tokens + 8, :] = rim.astype(F32)
    for c in range(tokens // TILE):
        planes = [pre[a, c * TILE : (c + 1) * TILE + 16, :] for a in range(3)]
        done = depthwise(planes, conv_w_ref, conv_b, TILE)
        xs[0, c * TILE : (c + 1) * TILE, :] = done.astype(BF)
    prepare(0)
    local(1)
    scan(1)
    local(0)
    scan(0)
    finish(1)
    start_all(c_copy)
    col_in[pl.ds(me, 1)] = col_out[pl.ds(me, 1)]
    finish(0)
    wait_all(c_copy)
    for c in range(tokens // TILE):
        rows = slice(c * TILE, (c + 1) * TILE)
        per = TILE // band
        col = col_in[c * per : (c + 1) * per].astype(F32).reshape(TILE, inner)
        gated = (own[0, rows, :] + col) * gate[rows, :]
        mean_square = jnp.mean(gated * gated, axis=-1, keepdims=True)
        normy = (gated * lax.rsqrt(mean_square + EPSILON) * out_gain).astype(BF)
        out_ref[0, :, rows] = (
            region_ref[:, rows].astype(F32) + mm_nt(out_w_ref[...], normy)
        ).astype(BF)
    wait_sent(r_copy)
    for p in range(2):
        wait_sent(functools.partial(s_copy, p))
        wait_sent(functools.partial(e_copy, p))
    wait_sent(c_copy)


def body(n, *args):
    region = args[0]
    _, tokens, width = region.shape
    inner = args[11].shape[0]
    groups = args[7].shape[0]
    heads = groups // 4
    state = args[5].shape[1] // 8
    band = tokens // n
    part = state // n
    block = max(TILE, 16 * n)
    count = tokens // block
    fold = TILE // band
    cell_rows = (width // fold + 8 + 15) // 16 * 16
    flat = [v if v.ndim > 1 else v.reshape(1, -1) for v in args]
    for i in (4, 10):
        if args[i].shape[0] % TILE == 0:
            flat[i] = args[i].reshape(-1, TILE)
    flat[0] = jnp.swapaxes(region, 1, 2)
    flat[6] = flat[6].T
    flat[11] = flat[11].T
    ent_rows = max(16, 2 * part)
    dma = pltpu.SemaphoreType.DMA
    vmem = pltpu.VMEM
    in_hbm = (0, 2, 3, 5, 6, 11)
    out = pl.pallas_call(
        functools.partial(kernel, n, heads, state, block),
        out_shape=jax.ShapeDtypeStruct(flat[0].shape, BF),
        in_specs=[
            pl.BlockSpec(memory_space=pltpu.HBM if i in in_hbm else pltpu.VMEM)
            for i in range(len(flat))
        ],
        out_specs=pl.BlockSpec(memory_space=pltpu.VMEM),
        scratch_shapes=[
            vmem((width, tokens), BF),
            *[vmem(flat[i].shape, flat[i].dtype) for i in in_hbm[1:]],
            vmem((n, cell_rows, TILE), BF),
            vmem((n, cell_rows, TILE), BF),
            vmem((2, width, tokens), BF),
            vmem((3, tokens + 16, inner), F32),
            vmem((n + 2, band + 16, inner), F32),
            vmem((tokens, inner), F32),
            vmem((2, tokens, inner), BF),
            vmem((2, tokens, 4 * state), BF),
            vmem((2, groups, tokens), F32),
            vmem((2, groups, tokens), F32),
            vmem((2, 2, count, state, inner), F32),
            vmem((2, 8, 2 * inner), F32),
            vmem((2, tokens, 2 * inner), F32),
            vmem((2, tokens, inner), F32),
            vmem((2, n, ent_rows, inner + TILE), BF),
            vmem((2, n, ent_rows, inner + TILE), BF),
            vmem((2, n, ent_rows, inner), BF),
            vmem((2, n, ent_rows, inner), BF),
            vmem((n, band, inner), BF),
            vmem((n, band, inner), BF),
            dma((6,)),
            dma((n,)),
            dma((n,)),
            dma((2,)),
            dma((2,)),
            dma((2, n)),
            dma((2, n)),
            dma((2, n)),
            dma((2, n)),
            dma((n,)),
            dma((n,)),
        ],
        compiler_params=pltpu.CompilerParams(
            collective_id=0, has_side_effects=True, vmem_limit_bytes=57 * 1024 * 1024
        ),
    )(*flat)
    return jnp.swapaxes(out, 1, 2)


def solution(mesh):
    in_specs = (P(("dp", "seq"), None, None),) + (P(),) * 11
    return jax.shard_map(
        functools.partial(body, mesh.shape["seq"]),
        mesh=mesh,
        in_specs=in_specs,
        out_specs=P(("dp", "seq"), None, None),
        check_vma=False,
    )
```

```python
import functools
import math
import jax
import jax.numpy as jnp
from jax import lax
from jax.experimental import pallas as pl
from jax.experimental.pallas import tpu as pltpu
from jax.sharding import PartitionSpec as P

EPSILON = 1e-05
BF = jnp.bfloat16
F32 = jnp.float32
TILE = 128
LOG2E = math.log2(math.e)


def mm(a, b):
    return jnp.dot(a, b, preferred_element_type=F32)


def mm_nt(a, b):
    return lax.dot_general(a, b, (((1,), (1,)), ((), ())), preferred_element_type=F32)


def mm_tn(a, b):
    return lax.dot_general(a, b, (((0,), (0,)), ((), ())), preferred_element_type=F32)


def split(v, count):
    pieces = []
    for _ in range(count):
        piece = v.astype(BF).astype(F32)
        pieces.append(piece)
        v = v - piece
    return jnp.concatenate(pieces, axis=0).astype(BF)


def iota(shape, dim):
    return lax.broadcasted_iota(jnp.int32, shape, dim)


def silu(v):
    half = 0.5 * v
    return half * jnp.tanh(half) + half


def depthwise(planes, weights, bias, size):
    sums = []
    for b in range(3):
        total = planes[0] * weights[b : b + 1, :]
        for a in (1, 2):
            tap = 3 * a + b
            total = total + planes[a] * weights[tap : tap + 1, :]
        sums.append(total)
    rows = sums[0].shape[0]
    moved = pltpu.roll(sums[0], 1, 0) + pltpu.roll(sums[2], rows - 1, 0)
    return silu((sums[1] + moved)[8 : 8 + size] + bias)


def bits(v):
    return v.bit_length() - 1


def one_row(ref):
    return jnp.concatenate([ref[i : i + 1, :] for i in range(ref.shape[0])], axis=1)


def roll_lanes(v, shift):
    shift = shift % v.shape[1]
    return v if shift == 0 else pltpu.roll(v, shift, 1)


def kernel(
    n,
    heads,
    state,
    block,
    region_hbm,
    norm_gain_hbm,
    in_w_hbm,
    conv_w_hbm,
    conv_b_hbm,
    coup_w_hbm,
    step_w_hbm,
    step_b_hbm,
    decay_hbm,
    skip_hbm,
    out_gain_hbm,
    out_w_hbm,
    out_ref,
    region_ref,
    norm_gain_ref,
    in_w_ref,
    conv_w_ref,
    conv_b_ref,
    coup_w_ref,
    step_w_ref,
    step_b_ref,
    decay_ref,
    skip_ref,
    out_gain_ref,
    out_w_ref,
    cells,
    got_cells,
    halo,
    pre,
    pcol,
    gate,
    xs,
    coup,
    cum,
    step_t,
    contrib,
    fade,
    grown,
    own,
    msg,
    got,
    ent_out,
    ent_in,
    col_out,
    col_in,
    local_sem,
    r_send,
    r_recv,
    halo_send,
    halo_recv,
    s_send,
    s_recv,
    e_send,
    e_recv,
    c_send,
    c_recv,
):
    me = lax.axis_index("seq")
    width, tokens = region_ref.shape
    inner = out_w_ref.shape[1]
    band = tokens // n
    head = inner // heads
    part = state // n
    groups = 4 * heads
    count = tokens // block
    span = block // n
    fold = TILE // band
    slab = width // fold
    edge_row = slab

    ring = [(k, lax.rem(me + k, n), lax.rem(me + n - k, n)) for k in range(1, n)]

    barrier = pltpu.get_barrier_semaphore()

    for _, peer, _ in ring:
        pl.semaphore_signal(barrier, inc=1, device_id={"seq": peer})

    sources = (
        region_hbm.at[0],
        norm_gain_hbm,
        in_w_hbm,
        conv_w_hbm,
        conv_b_hbm,
        coup_w_hbm,
        step_w_hbm,
        step_b_hbm,
        decay_hbm,
        skip_hbm,
        out_gain_hbm,
        out_w_hbm,
    )
    targets = (
        region_ref,
        norm_gain_ref,
        in_w_ref,
        conv_w_ref,
        conv_b_ref,
        coup_w_ref,
        step_w_ref,
        step_b_ref,
        decay_ref,
        skip_ref,
        out_gain_ref,
        out_w_ref,
    )
    fetch = [
        pltpu.make_async_copy(source, target, local_sem.at[i])
        for i, (source, target) in enumerate(zip(sources, targets))
    ]
    for copy in fetch:
        copy.start()

    def r_copy(k, chunk, place):
        return pltpu.make_async_remote_copy(
            src_ref=cells.at[chunk],
            dst_ref=got_cells.at[place],
            send_sem=r_send.at[k],
            recv_sem=r_recv.at[k],
            device_id={"seq": chunk},
        )

    def halo_copy(slot, device):
        return pltpu.make_async_remote_copy(
            src_ref=region_ref,
            dst_ref=halo.at[slot],
            send_sem=halo_send.at[slot],
            recv_sem=halo_recv.at[slot],
            device_id={"seq": device},
        )

    def s_copy(p, k, chunk, place):
        return pltpu.make_async_remote_copy(
            src_ref=msg.at[p, chunk],
            dst_ref=got.at[p, place],
            send_sem=s_send.at[p, k],
            recv_sem=s_recv.at[p, k],
            device_id={"seq": chunk},
        )

    def e_copy(p, k, chunk, place):
        return pltpu.make_async_remote_copy(
            src_ref=ent_out.at[p, chunk],
            dst_ref=ent_in.at[p, place],
            send_sem=e_send.at[p, k],
            recv_sem=e_recv.at[p, k],
            device_id={"seq": chunk},
        )

    def c_copy(k, chunk, place):
        return pltpu.make_async_remote_copy(
            src_ref=col_out.at[chunk],
            dst_ref=col_in.at[place],
            send_sem=c_send.at[k],
            recv_sem=c_recv.at[k],
            device_id={"seq": chunk},
        )

    def start_all(make, partners=ring):
        for k, peer, _ in partners:
            make(k, peer, me).start()

    def wait_all(make, partners=ring):
        for k, peer, source in partners:
            make(k, peer, source).wait_recv()

    def wait_sent(make, partners=ring):
        for k, peer, source in partners:
            make(k, peer, source).wait_send()

    piece = jnp.right_shift(iota((slab, TILE), 1), bits(band))
    fetch[0].wait()
    rest = cells.shape[1] - slab - 8
    sel_row = iota((8 * n, tokens), 0)
    sel_band = jnp.right_shift(sel_row, 3)
    sel_kind = jnp.bitwise_and(sel_row, 7)
    sel_cell = iota((8 * n, tokens), 1)
    side = jnp.where(
        jnp.bitwise_and(sel_kind, 1) == 0, sel_band * band - 1, sel_band * band + band
    )
    hit = sel_cell == side
    low = jnp.where(hit & (sel_kind < 2), 1.0, 0.0).astype(BF)
    high = jnp.where(hit & (sel_kind >= 2) & (sel_kind < 4), 1.0, 0.0).astype(BF)
    edges = mm_nt(low, region_ref[0:TILE, :]) + mm_nt(high, region_ref[width - TILE : width, :])
    for m in range(tokens // TILE):
        lanes = region_ref[:, m * TILE : (m + 1) * TILE].astype(F32)
        for r in range(fold):
            packed = lanes[0:slab]
            packed = roll_lanes(packed, (0 - r) * band)
            for q in range(1, fold):
                moved = roll_lanes(lanes[q * slab : (q + 1) * slab], (q - r) * band)
                packed = jnp.where(piece == q, moved, packed)
            d = m * fold + r
            parts = [packed, edges[8 * d : 8 * d + 8]]
            if rest:
                parts.append(jnp.zeros((rest, TILE), F32))
            cells[d] = jnp.concatenate(parts, axis=0).astype(BF)

    pl.semaphore_wait(barrier, n - 1)
    start_all(r_copy)

    @pl.when(me < n - 1)
    def _():
        halo_copy(0, me + 1).start()

    @pl.when(me > 0)
    def _():
        halo_copy(1, me - 1).start()

    got_cells[pl.ds(me, 1)] = cells[pl.ds(me, 1)]

    for copy in fetch[1:]:
        copy.wait()
    gain_row = norm_gain_ref[...]
    conv_b = one_row(conv_b_ref)
    out_gain = one_row(out_gain_ref)
    gain_col = jnp.broadcast_to(gain_row, (8, width)).T[:, 0:1]

    def normed(values):
        mean_square = jnp.mean(values * values, axis=0, keepdims=True)
        return (values * lax.rsqrt(mean_square + EPSILON) * gain_col).astype(BF)

    edge = jnp.zeros((8, inner), F32)
    for a in range(3):
        pre[a, 0:8, :] = edge
        pre[a, tokens + 8 : tokens + 16, :] = edge
    blank = jnp.zeros((band + 16, inner), F32)
    pcol[0] = blank
    pcol[n + 1] = blank
    mine = mm_tn(normed(region_ref[...].astype(F32)), in_w_ref[...]).astype(BF)
    pre[1, 8 : tokens + 8, :] = mine[:, :inner].astype(F32)
    gate[...] = silu(mine[:, inner:].astype(F32))

    wait_all(r_copy)

    for m in range(tokens // TILE):
        slabs = []
        for q in range(fold):
            packed = None
            for r in range(fold):
                moved = roll_lanes(
                    got_cells[m * fold + r, 0:slab, :].astype(F32), (r - q) * band
                )
                packed = moved if packed is None else jnp.where(piece == r, moved, packed)
            slabs.append(packed)
        values = normed(jnp.concatenate(slabs, axis=0))
        done = mm_tn(values, in_w_ref[:, :inner]).astype(BF).astype(F32)
        for r in range(fold):
            pcol[m * fold + r + 1, 8 : band + 8, :] = done[r * band : (r + 1) * band]
    rims = jnp.concatenate(
        [got_cells[i, edge_row : cells.shape[1], :].astype(F32)[0:8] for i in range(n)], axis=0
    )
    rim_low = rims
    rim_high = jnp.where(
        iota((8 * n, TILE), 1) >= 2 * TILE - width, pltpu.roll(rims, 8 * n - 2, 0), 0.0
    )
    mean_square = (
        jnp.sum(rim_low * rim_low, axis=-1, keepdims=True)
        + jnp.sum(rim_high * rim_high, axis=-1, keepdims=True)
    ) / width
    scale = lax.rsqrt(mean_square + EPSILON)
    rim_pre = mm(
        (rim_low * scale * gain_row[:, 0:TILE]).astype(BF), in_w_ref[0:TILE, :inner]
    ) + mm(
        (rim_high * scale * gain_row[:, width - TILE : width]).astype(BF),
        in_w_ref[width - TILE : width, :inner],
    )
    rim_pre = rim_pre.astype(BF).astype(F32)
    for i in range(n):
        pcol[i + 1, 7:8, :] = rim_pre[8 * i : 8 * i + 1]
        pcol[i + 1, band + 8 : band + 9, :] = rim_pre[8 * i + 1 : 8 * i + 2]
    for i in range(n):
        planes = [pcol[i + a] for a in range(3)]
        done = depthwise(planes, conv_w_ref, conv_b, band).astype(BF)
        for c in range(count):
            start = c * block + i * span
            xs[1, start : start + span, :] = done[c * span : (c + 1) * span]

    group = iota((groups, 1), 0)
    behind_group = lax.rem(group, 2 * heads) >= heads
    behind_lane = lax.rem(iota((1, groups), 1), 2 * heads) >= heads
    eye = iota((groups, groups), 0) == iota((groups, groups), 1)

    def column_of(row):
        return jnp.sum(jnp.where(eye, row, 0.0), axis=1, keepdims=True)

    def row_of(column):
        here = iota((groups, TILE), 0) == iota((groups, TILE), 1)
        return jnp.sum(jnp.where(here, column, 0.0), axis=0, keepdims=True)

    rates = -jnp.exp(column_of(decay_ref[...]))
    step_b = column_of(step_b_ref[...])
    skips = column_of(skip_ref[...])

    def spreader(p):
        where = jnp.right_shift(iota((groups, 2 * inner), 1), bits(head))
        return (iota((groups, 2 * inner), 0) == where + p * 2 * heads).astype(F32)

    def spread(v, e, pieces):
        many = jnp.concatenate([e] * pieces, axis=0).astype(BF)
        return mm_tn(split(v, pieces), many)

    def position(p, v):
        if p == 0:
            return v
        return jnp.bitwise_and(v, span - 1) * n + jnp.right_shift(v, bits(span))

    def rows_of(c):
        return slice(c * block, (c + 1) * block)

    def prepare(p):
        x = xs[p]
        first = p * 4 * state
        coup[p] = mm(x, coup_w_ref[:, first : first + 4 * state]).astype(BF)
        logits = mm_nt(step_w_ref[...], x) + step_b
        steps = jnp.maximum(logits, 0.0) + jnp.log1p(jnp.exp(-jnp.abs(logits)))
        logs = rates * steps
        step_t[p] = steps
        pieces = split(logs, 3)
        earlier = position(p, iota((block, block), 0)) <= position(p, iota((block, block), 1))
        earlier = jnp.where(earlier, 1.0, 0.0).astype(BF)
        e = spreader(p)
        lane = iota((groups, TILE), 1)
        totals = jnp.zeros((groups, TILE), F32)
        whole = jnp.zeros((groups, 1), F32)
        for c in range(count):
            rows = rows_of(c)
            sums = mm(pieces[:, rows], earlier)
            ahead = sums[0:groups] + sums[groups : 2 * groups] + sums[2 * groups : 3 * groups]
            total = ahead[:, block - 1 : block]
            level = jnp.where(behind_group, total - ahead + logs[:, rows], ahead)
            cum[p, :, rows] = level
            totals = jnp.where(lane == c, total, totals)
            whole = whole + total
            tails = spread(jnp.exp(total - level) * steps[:, rows], e, 2)
            xf = xs[p, rows, :].astype(F32)
            for o in range(2):
                weighted = (xf * tails[:, o * inner : (o + 1) * inner]).astype(BF)
                writer = coup[p, rows, 2 * o * state : (2 * o + 1) * state]
                contrib[p, o, c] = mm_tn(writer, weighted)
        left = row_of(whole)
        line = iota((msg.shape[2], TILE), 0)
        totals_sent = jnp.zeros((msg.shape[2], TILE), F32)
        for i in range(3):
            rounded = left.astype(BF).astype(F32)
            totals_sent = jnp.where(line == i, rounded, totals_sent)
            left = left - rounded
        totals_sent = totals_sent.astype(BF)
        fade[p] = spread(jnp.exp(totals), e, 3)[0:8]
        sums = [contrib[p, 0, 0], contrib[p, 1, count - 1]]
        for c in range(1, count):
            sums[0] = fade[p, c : c + 1, :inner] * sums[0] + contrib[p, 0, c]
            back = count - 1 - c
            sums[1] = fade[p, back : back + 1, inner:] * sums[1] + contrib[p, 1, back]
        for d in range(n):
            pieces = [v[d * part : (d + 1) * part] for v in sums]
            if 2 * part < 16:
                pieces.append(jnp.zeros((16 - 2 * part, inner), F32))
            msg[p, d, :, 0:inner] = jnp.concatenate(pieces, axis=0).astype(BF)
            msg[p, d, :, inner:] = totals_sent
        start_all(functools.partial(s_copy, p))
        got[p, pl.ds(me, 1)] = msg[p, pl.ds(me, 1)]

    def local(p):
        e = spreader(p)
        both_sides = e[:, :inner] + e[:, inner:]
        eyes = eye.astype(F32)
        rows_tile = min(block, TILE)
        even = jnp.bitwise_and(iota((1, 2 * head), 1), head) == 0
        for c in range(count):
            rows = rows_of(c)
            level = cum[p, :, rows]
            steps = step_t[p, :, rows]
            grown[p, rows, :] = spread(jnp.exp(level), e, 2)
            scaled = level * LOG2E
            source = scaled - jnp.log(steps) * LOG2E
            target = spread(scaled, eyes, 3)
            xf = xs[p, rows, :].astype(F32)
            pairs = []
            for j in range(heads // 2):
                lanes = xf[:, 2 * j * head : 2 * (j + 1) * head]
                pairs.append(
                    jnp.concatenate(
                        [jnp.where(even, lanes, 0.0), jnp.where(even, 0.0, lanes)], axis=0
                    ).astype(BF)
                )
            diagonals = [jnp.zeros((1, block), F32)] * 2
            for q in range(block // rows_tile):
                t0 = q * rows_tile
                mine = coup[p, c * block + t0 : c * block + t0 + rows_tile, :]
                ahead = mm_nt(mine[:, state : 2 * state], coup[p, rows, 0:state])
                behind = mm_nt(mine[:, 3 * state :], coup[p, rows, 2 * state : 3 * state])
                t = iota((rows_tile, block), 0) + t0
                s = iota((rows_tile, block), 1)
                after = position(p, t) > position(p, s)
                same = t == s
                scores = jnp.where(same, 0.0, jnp.where(after, ahead, behind))
                for o, v in enumerate((ahead, behind)):
                    found = jnp.sum(jnp.where(same, v, 0.0), axis=0, keepdims=True)
                    diagonals[o] = diagonals[o] + found

                def weights(h):
                    f = p * 2 * heads + h
                    g = f + heads
                    lead = target[t0 : t0 + rows_tile, f : f + 1] - source[f : f + 1, :]
                    back = target[t0 : t0 + rows_tile, g : g + 1] - source[g : g + 1, :]
                    return (scores * jnp.exp2(jnp.where(after, lead, back))).astype(BF)

                for j in range(heads // 2):
                    pair = jnp.concatenate([weights(2 * j), weights(2 * j + 1)], axis=1)
                    own[
                        p,
                        c * block + t0 : c * block + t0 + rows_tile,
                        2 * j * head : 2 * (j + 1) * head,
                    ] = mm(pair, pairs[j])
            diag = jnp.where(behind_group, diagonals[1], diagonals[0]) * steps
            diag = diag.astype(BF).astype(F32) + skips
            own[p, rows, :] += xf * spread(diag, both_sides, 2)

    def scan(p):
        wait_all(functools.partial(s_copy, p))
        e = spreader(p)
        logs = jnp.concatenate(
            [got[p, i, :, inner:].astype(F32)[0:8] for i in range(n)], axis=0
        )
        logs = logs + pltpu.roll(logs, 8 * n - 1, 0) + pltpu.roll(logs, 8 * n - 2, 0)
        pieces = split(jnp.exp(logs[:, 0:groups]), 3).reshape(3, 8 * n, groups)
        fades = sum(mm(pieces[i], e.astype(BF)) for i in range(3))
        entry = jnp.zeros((part, inner), F32)
        ahead = []
        for i in range(n):
            ahead.append(entry)
            entry = fades[8 * i : 8 * i + 1, :inner] * entry + got[p, i, :, 0:inner].astype(F32)[0:part]
        entry = jnp.zeros((part, inner), F32)
        for i in reversed(range(n)):
            pieces = [ahead[i], entry]
            if 2 * part < 16:
                pieces.append(jnp.zeros((16 - 2 * part, inner), F32))
            ent_out[p, i] = jnp.concatenate(pieces, axis=0).astype(BF)
            entry = (
                fades[8 * i : 8 * i + 1, inner:] * entry + got[p, i, :, 0:inner].astype(F32)[part : 2 * part]
            )
        start_all(functools.partial(e_copy, p))
        ent_in[p, pl.ds(me, 1)] = ent_out[p, pl.ds(me, 1)]

    def finish(p):
        wait_all(functools.partial(e_copy, p))
        arrived = [ent_in[p, i].astype(F32) for i in range(n)]
        entries = [[None] * count, [None] * count]
        for o in range(2):
            entry = jnp.concatenate([v[o * part : (o + 1) * part] for v in arrived], axis=0)
            order = range(count) if o == 0 else reversed(range(count))
            for c in order:
                entries[o][c] = entry.astype(BF)
                lanes = slice(o * inner, (o + 1) * inner)
                entry = fade[p, c : c + 1, lanes] * entry + contrib[p, o, c]
        for c in range(count):
            rows = rows_of(c)
            result = own[p, rows, :]
            for o in range(2):
                reader = coup[p, rows, (2 * o + 1) * state : (2 * o + 2) * state]
                carried = mm(reader, entries[o][c])
                result = result + carried * grown[p, rows, o * inner : (o + 1) * inner]
            if p == 0:
                own[p, rows, :] = result
            else:
                result = result.astype(BF)
                for i in range(n):
                    col_out[i, c * span : (c + 1) * span, :] = result[i * span : (i + 1) * span]

    prepare(1)
    @pl.when(me < n - 1)
    def _():
        halo_copy(1, me + 1).wait_recv()
        halo_copy(0, me + 1).wait_send()

    @pl.when(me == n - 1)
    def _():
        halo[1] = jnp.zeros((width, tokens), BF)

    @pl.when(me > 0)
    def _():
        halo_copy(0, me - 1).wait_recv()
        halo_copy(1, me - 1).wait_send()

    @pl.when(me == 0)
    def _():
        halo[0] = jnp.zeros((width, tokens), BF)

    for slot, a in ((0, 0), (1, 2)):
        rim = mm_tn(normed(halo[slot].astype(F32)), in_w_ref[:, :inner]).astype(BF)
        pre[a, 8 : tokens + 8, :] = rim.astype(F32)
    for c in range(tokens // TILE):
        planes = [pre[a, c * TILE : (c + 1) * TILE + 16, :] for a in range(3)]
        done = depthwise(planes, conv_w_ref, conv_b, TILE)
        xs[0, c * TILE : (c + 1) * TILE, :] = done.astype(BF)
    prepare(0)
    scan(1)
    local(1)
    scan(0)
    finish(1)
    start_all(c_copy)
    col_in[pl.ds(me, 1)] = col_out[pl.ds(me, 1)]
    local(0)
    finish(0)
    wait_all(c_copy)
    for c in range(tokens // TILE):
        rows = slice(c * TILE, (c + 1) * TILE)
        per = TILE // band
        col = col_in[c * per : (c + 1) * per].astype(F32).reshape(TILE, inner)
        gated = (own[0, rows, :] + col) * gate[rows, :]
        mean_square = jnp.mean(gated * gated, axis=-1, keepdims=True)
        normy = (gated * lax.rsqrt(mean_square + EPSILON) * out_gain).astype(BF)
        out_ref[0, :, rows] = (
            region_ref[:, rows].astype(F32) + mm_nt(out_w_ref[...], normy)
        ).astype(BF)
    wait_sent(r_copy)
    for p in range(2):
        wait_sent(functools.partial(s_copy, p))
        wait_sent(functools.partial(e_copy, p))
    wait_sent(c_copy)


def body(n, *args):
    region = args[0]
    _, tokens, width = region.shape
    inner = args[11].shape[0]
    groups = args[7].shape[0]
    heads = groups // 4
    state = args[5].shape[1] // 8
    band = tokens // n
    part = state // n
    block = max(TILE, 16 * n)
    count = tokens // block
    fold = TILE // band
    cell_rows = (width // fold + 8 + 15) // 16 * 16
    flat = [v if v.ndim > 1 else v.reshape(1, -1) for v in args]
    for i in (4, 10):
        if args[i].shape[0] % TILE == 0:
            flat[i] = args[i].reshape(-1, TILE)
    flat[0] = jnp.swapaxes(region, 1, 2)
    flat[6] = flat[6].T
    flat[11] = flat[11].T
    ent_rows = max(16, 2 * part)
    dma = pltpu.SemaphoreType.DMA
    vmem = pltpu.VMEM
    flat = [pltpu.with_memory_space_constraint(v, pltpu.HBM) for v in flat]
    out = pl.pallas_call(
        functools.partial(kernel, n, heads, state, block),
        out_shape=jax.ShapeDtypeStruct(flat[0].shape, BF),
        in_specs=[pl.BlockSpec(memory_space=pltpu.HBM)] * len(flat),
        out_specs=pl.BlockSpec(memory_space=pltpu.VMEM),
        scratch_shapes=[
            vmem((width, tokens), BF),
            *[vmem(v.shape, v.dtype) for v in flat[1:]],
            vmem((n, cell_rows, TILE), BF),
            vmem((n, cell_rows, TILE), BF),
            vmem((2, width, tokens), BF),
            vmem((3, tokens + 16, inner), F32),
            vmem((n + 2, band + 16, inner), F32),
            vmem((tokens, inner), F32),
            vmem((2, tokens, inner), BF),
            vmem((2, tokens, 4 * state), BF),
            vmem((2, groups, tokens), F32),
            vmem((2, groups, tokens), F32),
            vmem((2, 2, count, state, inner), F32),
            vmem((2, 8, 2 * inner), F32),
            vmem((2, tokens, 2 * inner), F32),
            vmem((2, tokens, inner), F32),
            vmem((2, n, ent_rows, inner + TILE), BF),
            vmem((2, n, ent_rows, inner + TILE), BF),
            vmem((2, n, ent_rows, inner), BF),
            vmem((2, n, ent_rows, inner), BF),
            vmem((n, band, inner), BF),
            vmem((n, band, inner), BF),
            dma((len(flat),)),
            dma((n,)),
            dma((n,)),
            dma((2,)),
            dma((2,)),
            dma((2, n)),
            dma((2, n)),
            dma((2, n)),
            dma((2, n)),
            dma((n,)),
            dma((n,)),
        ],
        compiler_params=pltpu.CompilerParams(
            collective_id=0, has_side_effects=True, vmem_limit_bytes=40 * 1024 * 1024
        ),
    )(*flat)
    return jnp.swapaxes(out, 1, 2)


def solution(mesh):
    in_specs = (P(("dp", "seq"), None, None),) + (P(),) * 11
    return jax.shard_map(
        functools.partial(body, mesh.shape["seq"]),
        mesh=mesh,
        in_specs=in_specs,
        out_specs=P(("dp", "seq"), None, None),
        check_vma=False,
    )
```

```python
import functools
import math
import jax
import jax.numpy as jnp
from jax import lax
from jax.experimental import pallas as pl
from jax.experimental.pallas import tpu as pltpu
from jax.sharding import PartitionSpec as P

EPSILON = 1e-05
BF = jnp.bfloat16
F32 = jnp.float32
TILE = 128
LOG2E = math.log2(math.e)


def mm(a, b):
    return jnp.dot(a, b, preferred_element_type=F32)


def mm_nt(a, b):
    return lax.dot_general(a, b, (((1,), (1,)), ((), ())), preferred_element_type=F32)


def mm_tn(a, b):
    return lax.dot_general(a, b, (((0,), (0,)), ((), ())), preferred_element_type=F32)


def split(v, count):
    pieces = []
    for _ in range(count):
        piece = v.astype(BF).astype(F32)
        pieces.append(piece)
        v = v - piece
    return jnp.concatenate(pieces, axis=0).astype(BF)


def iota(shape, dim):
    return lax.broadcasted_iota(jnp.int32, shape, dim)


def silu(v):
    half = 0.5 * v
    return half * jnp.tanh(half) + half


def depthwise(load, weights, bias, size):
    parts = []
    for q in range(weights.shape[1] // TILE):
        lanes = slice(q * TILE, (q + 1) * TILE)
        planes = [load(a, lanes) for a in range(3)]
        sums = []
        for b, first, last in ((0, 0, size + 8), (1, 8, size + 8), (2, 8, size + 16)):
            total = planes[0][first:last] * weights[b : b + 1, lanes]
            for a in (1, 2):
                tap = 3 * a + b
                total = total + planes[a][first:last] * weights[tap : tap + 1, lanes]
            sums.append(total)
        left = pltpu.roll(sums[0], 1, 0)[8:]
        right = pltpu.roll(sums[2], size + 7, 0)[:size]
        parts.append(silu(sums[1] + bias[:, lanes] + (left + right)))
    return jnp.concatenate(parts, axis=1)


def bits(v):
    return v.bit_length() - 1


def one_row(ref):
    return jnp.concatenate([ref[i : i + 1, :] for i in range(ref.shape[0])], axis=1)


def roll_lanes(v, shift):
    shift = shift % v.shape[1]
    return v if shift == 0 else pltpu.roll(v, shift, 1)


def kernel(
    n,
    heads,
    state,
    block,
    region_hbm,
    norm_gain_hbm,
    in_w_hbm,
    conv_w_hbm,
    conv_b_hbm,
    coup_w_hbm,
    step_w_hbm,
    step_b_hbm,
    decay_hbm,
    skip_hbm,
    out_gain_hbm,
    out_w_hbm,
    out_ref,
    region_ref,
    norm_gain_ref,
    in_w_ref,
    conv_w_ref,
    conv_b_ref,
    coup_w_ref,
    step_w_ref,
    step_b_ref,
    decay_ref,
    skip_ref,
    out_gain_ref,
    out_w_ref,
    cells,
    got_cells,
    halo,
    pre,
    pcol,
    gate,
    xs,
    coup,
    cum,
    step_t,
    contrib,
    fade,
    grown,
    own,
    msg,
    got,
    ent_out,
    ent_in,
    col_out,
    col_in,
    local_sem,
    r_send,
    r_recv,
    halo_send,
    halo_recv,
    s_send,
    s_recv,
    e_send,
    e_recv,
    c_send,
    c_recv,
):
    me = lax.axis_index("seq")
    width, tokens = region_ref.shape
    inner = out_w_ref.shape[1]
    band = tokens // n
    head = inner // heads
    part = state // n
    groups = 4 * heads
    count = tokens // block
    span = block // n
    fold = TILE // band
    slab = width // fold
    edge_row = slab

    ring = [(k, lax.rem(me + k, n), lax.rem(me + n - k, n)) for k in range(1, n)]

    barrier = pltpu.get_barrier_semaphore()

    for _, peer, _ in ring:
        pl.semaphore_signal(barrier, inc=1, device_id={"seq": peer})

    sources = (
        region_hbm.at[0],
        norm_gain_hbm,
        in_w_hbm,
        conv_w_hbm,
        conv_b_hbm,
        coup_w_hbm,
        step_w_hbm,
        step_b_hbm,
        decay_hbm,
        skip_hbm,
        out_gain_hbm,
        out_w_hbm,
    )
    targets = (
        region_ref,
        norm_gain_ref,
        in_w_ref,
        conv_w_ref,
        conv_b_ref,
        coup_w_ref,
        step_w_ref,
        step_b_ref,
        decay_ref,
        skip_ref,
        out_gain_ref,
        out_w_ref,
    )
    fetch = [
        pltpu.make_async_copy(source, target, local_sem.at[i])
        for i, (source, target) in enumerate(zip(sources, targets))
    ]
    for copy in fetch:
        copy.start()

    def r_copy(k, chunk, place):
        return pltpu.make_async_remote_copy(
            src_ref=cells.at[chunk],
            dst_ref=got_cells.at[place],
            send_sem=r_send.at[k],
            recv_sem=r_recv.at[k],
            device_id={"seq": chunk},
        )

    def halo_copy(slot, device):
        return pltpu.make_async_remote_copy(
            src_ref=region_ref,
            dst_ref=halo.at[slot],
            send_sem=halo_send.at[slot],
            recv_sem=halo_recv.at[slot],
            device_id={"seq": device},
        )

    def s_copy(p, k, chunk, place):
        return pltpu.make_async_remote_copy(
            src_ref=msg.at[p, chunk],
            dst_ref=got.at[p, place],
            send_sem=s_send.at[p, k],
            recv_sem=s_recv.at[p, k],
            device_id={"seq": chunk},
        )

    def e_copy(p, k, chunk, place):
        return pltpu.make_async_remote_copy(
            src_ref=ent_out.at[p, chunk],
            dst_ref=ent_in.at[p, place],
            send_sem=e_send.at[p, k],
            recv_sem=e_recv.at[p, k],
            device_id={"seq": chunk},
        )

    def c_copy(k, chunk, place):
        return pltpu.make_async_remote_copy(
            src_ref=col_out.at[chunk],
            dst_ref=col_in.at[place],
            send_sem=c_send.at[k],
            recv_sem=c_recv.at[k],
            device_id={"seq": chunk},
        )

    def start_all(make, partners=ring):
        for k, peer, _ in partners:
            make(k, peer, me).start()

    def wait_all(make, partners=ring):
        for k, peer, source in partners:
            make(k, peer, source).wait_recv()

    def wait_sent(make, partners=ring):
        for k, peer, source in partners:
            make(k, peer, source).wait_send()

    piece = jnp.right_shift(iota((slab, TILE), 1), bits(band))
    fetch[0].wait()
    rest = cells.shape[1] - slab - 8
    sel_row = iota((8 * n, tokens), 0)
    sel_band = jnp.right_shift(sel_row, 3)
    sel_kind = jnp.bitwise_and(sel_row, 7)
    sel_cell = iota((8 * n, tokens), 1)
    side = jnp.where(
        jnp.bitwise_and(sel_kind, 1) == 0, sel_band * band - 1, sel_band * band + band
    )
    hit = sel_cell == side
    low = jnp.where(hit & (sel_kind < 2), 1.0, 0.0).astype(BF)
    high = jnp.where(hit & (sel_kind >= 2) & (sel_kind < 4), 1.0, 0.0).astype(BF)
    edges = mm_nt(low, region_ref[0:TILE, :]) + mm_nt(high, region_ref[width - TILE : width, :])
    for m in range(tokens // TILE):
        lanes = region_ref[:, m * TILE : (m + 1) * TILE].astype(F32)
        for r in range(fold):
            packed = lanes[0:slab]
            packed = roll_lanes(packed, (0 - r) * band)
            for q in range(1, fold):
                moved = roll_lanes(lanes[q * slab : (q + 1) * slab], (q - r) * band)
                packed = jnp.where(piece == q, moved, packed)
            d = m * fold + r
            parts = [packed, edges[8 * d : 8 * d + 8]]
            if rest:
                parts.append(jnp.zeros((rest, TILE), F32))
            cells[d] = jnp.concatenate(parts, axis=0).astype(BF)

    pl.semaphore_wait(barrier, n - 1)
    start_all(r_copy)

    @pl.when(me < n - 1)
    def _():
        halo_copy(0, me + 1).start()

    @pl.when(me > 0)
    def _():
        halo_copy(1, me - 1).start()

    got_cells[pl.ds(me, 1)] = cells[pl.ds(me, 1)]

    for copy in fetch[1:]:
        copy.wait()
    gain_row = norm_gain_ref[...]
    conv_b = one_row(conv_b_ref)
    out_gain = one_row(out_gain_ref)
    gain_col = jnp.broadcast_to(gain_row, (8, width)).T[:, 0:1]

    def normed(values):
        mean_square = jnp.mean(values * values, axis=0, keepdims=True)
        return (values * lax.rsqrt(mean_square + EPSILON) * gain_col).astype(BF)

    edge = jnp.zeros((8, inner), F32)
    for a in range(3):
        pre[a, 0:8, :] = edge
        pre[a, tokens + 8 : tokens + 16, :] = edge
    blank = jnp.zeros((band + 16, inner), F32)
    pcol[0] = blank
    pcol[n + 1] = blank
    mine = mm_tn(normed(region_ref[...].astype(F32)), in_w_ref[...]).astype(BF)
    pre[1, 8 : tokens + 8, :] = mine[:, :inner].astype(F32)
    gate[...] = silu(mine[:, inner:].astype(F32))

    wait_all(r_copy)

    for m in range(tokens // TILE):
        slabs = []
        for q in range(fold):
            packed = None
            for r in range(fold):
                moved = roll_lanes(
                    got_cells[m * fold + r, 0:slab, :].astype(F32), (r - q) * band
                )
                packed = moved if packed is None else jnp.where(piece == r, moved, packed)
            slabs.append(packed)
        values = normed(jnp.concatenate(slabs, axis=0))
        done = mm_tn(values, in_w_ref[:, :inner]).astype(BF).astype(F32)
        for r in range(fold):
            pcol[m * fold + r + 1, 8 : band + 8, :] = done[r * band : (r + 1) * band]
    rims = jnp.concatenate(
        [got_cells[i, edge_row : cells.shape[1], :].astype(F32)[0:8] for i in range(n)], axis=0
    )
    rim_low = rims
    rim_high = jnp.where(
        iota((8 * n, TILE), 1) >= 2 * TILE - width, pltpu.roll(rims, 8 * n - 2, 0), 0.0
    )
    mean_square = (
        jnp.sum(rim_low * rim_low, axis=-1, keepdims=True)
        + jnp.sum(rim_high * rim_high, axis=-1, keepdims=True)
    ) / width
    scale = lax.rsqrt(mean_square + EPSILON)
    rim_pre = mm(
        (rim_low * scale * gain_row[:, 0:TILE]).astype(BF), in_w_ref[0:TILE, :inner]
    ) + mm(
        (rim_high * scale * gain_row[:, width - TILE : width]).astype(BF),
        in_w_ref[width - TILE : width, :inner],
    )
    rim_pre = rim_pre.astype(BF).astype(F32)
    for i in range(n):
        pcol[i + 1, 7:8, :] = rim_pre[8 * i : 8 * i + 1]
        pcol[i + 1, band + 8 : band + 9, :] = rim_pre[8 * i + 1 : 8 * i + 2]
    for i in range(n):
        done = depthwise(lambda a, lanes: pcol[i + a, :, lanes], conv_w_ref, conv_b, band).astype(BF)
        for c in range(count):
            start = c * block + i * span
            xs[1, start : start + span, :] = done[c * span : (c + 1) * span]

    group = iota((groups, 1), 0)
    behind_group = lax.rem(group, 2 * heads) >= heads
    behind_lane = lax.rem(iota((1, groups), 1), 2 * heads) >= heads
    eye = iota((groups, groups), 0) == iota((groups, groups), 1)

    def column_of(row):
        return jnp.sum(jnp.where(eye, row, 0.0), axis=1, keepdims=True)

    def row_of(column):
        here = iota((groups, TILE), 0) == iota((groups, TILE), 1)
        return jnp.sum(jnp.where(here, column, 0.0), axis=0, keepdims=True)

    rates = -jnp.exp(column_of(decay_ref[...]))
    step_b = column_of(step_b_ref[...])
    skips = column_of(skip_ref[...])

    def spreader(p):
        where = jnp.right_shift(iota((groups, 2 * inner), 1), bits(head))
        return (iota((groups, 2 * inner), 0) == where + p * 2 * heads).astype(F32)

    def spread(v, e, pieces):
        many = jnp.concatenate([e] * pieces, axis=0).astype(BF)
        return mm_tn(split(v, pieces), many)

    def position(p, v):
        if p == 0:
            return v
        return jnp.bitwise_and(v, span - 1) * n + jnp.right_shift(v, bits(span))

    def rows_of(c):
        return slice(c * block, (c + 1) * block)

    def prepare(p):
        x = xs[p]
        first = p * 4 * state
        coup[p] = mm(x, coup_w_ref[:, first : first + 4 * state]).astype(BF)
        logits = mm_nt(step_w_ref[...], x) + step_b
        steps = jnp.maximum(logits, 0.0) + jnp.log1p(jnp.exp(-jnp.abs(logits)))
        logs = rates * steps
        step_t[p] = steps
        pieces = split(logs, 3)
        earlier = position(p, iota((block, block), 0)) <= position(p, iota((block, block), 1))
        earlier = jnp.where(earlier, 1.0, 0.0).astype(BF)
        e = spreader(p)
        lane = iota((groups, TILE), 1)
        totals = jnp.zeros((groups, TILE), F32)
        whole = jnp.zeros((groups, 1), F32)
        for c in range(count):
            rows = rows_of(c)
            sums = mm(pieces[:, rows], earlier)
            ahead = sums[0:groups] + sums[groups : 2 * groups] + sums[2 * groups : 3 * groups]
            total = ahead[:, block - 1 : block]
            level = jnp.where(behind_group, total - ahead + logs[:, rows], ahead)
            cum[p, :, rows] = level
            totals = jnp.where(lane == c, total, totals)
            whole = whole + total
            tails = spread(jnp.exp(total - level) * steps[:, rows], e, 2)
            xf = xs[p, rows, :].astype(F32)
            for o in range(2):
                weighted = (xf * tails[:, o * inner : (o + 1) * inner]).astype(BF)
                writer = coup[p, rows, 2 * o * state : (2 * o + 1) * state]
                contrib[p, o, c] = mm_tn(writer, weighted)
        left = row_of(whole)
        line = iota((msg.shape[2], TILE), 0)
        totals_sent = jnp.zeros((msg.shape[2], TILE), F32)
        for i in range(3):
            rounded = left.astype(BF).astype(F32)
            totals_sent = jnp.where(line == i, rounded, totals_sent)
            left = left - rounded
        totals_sent = totals_sent.astype(BF)
        fade[p] = spread(jnp.exp(totals), e, 3)[0:8]
        sums = [contrib[p, 0, 0], contrib[p, 1, count - 1]]
        for c in range(1, count):
            sums[0] = fade[p, c : c + 1, :inner] * sums[0] + contrib[p, 0, c]
            back = count - 1 - c
            sums[1] = fade[p, back : back + 1, inner:] * sums[1] + contrib[p, 1, back]
        for d in range(n):
            pieces = [v[d * part : (d + 1) * part] for v in sums]
            if 2 * part < 16:
                pieces.append(jnp.zeros((16 - 2 * part, inner), F32))
            msg[p, d, :, 0:inner] = jnp.concatenate(pieces, axis=0).astype(BF)
            msg[p, d, :, inner:] = totals_sent
        start_all(functools.partial(s_copy, p))
        got[p, pl.ds(me, 1)] = msg[p, pl.ds(me, 1)]

    def local(p):
        e = spreader(p)
        both_sides = e[:, :inner] + e[:, inner:]
        eyes = eye.astype(F32)
        rows_tile = min(block, TILE)
        even = jnp.bitwise_and(iota((1, 2 * head), 1), head) == 0
        for c in range(count):
            rows = rows_of(c)
            level = cum[p, :, rows]
            steps = step_t[p, :, rows]
            grown[p, rows, :] = spread(jnp.exp(level), e, 2)
            scaled = level * LOG2E
            source = scaled - jnp.log(steps) * LOG2E
            target = spread(scaled, eyes, 3)
            xf = xs[p, rows, :].astype(F32)
            pairs = []
            for j in range(heads // 2):
                lanes = xf[:, 2 * j * head : 2 * (j + 1) * head]
                pairs.append(
                    jnp.concatenate(
                        [jnp.where(even, lanes, 0.0), jnp.where(even, 0.0, lanes)], axis=0
                    ).astype(BF)
                )
            diagonals = [jnp.zeros((1, block), F32)] * 2
            for q in range(block // rows_tile):
                t0 = q * rows_tile
                mine = coup[p, c * block + t0 : c * block + t0 + rows_tile, :]
                ahead = mm_nt(mine[:, state : 2 * state], coup[p, rows, 0:state])
                behind = mm_nt(mine[:, 3 * state :], coup[p, rows, 2 * state : 3 * state])
                t = iota((rows_tile, block), 0) + t0
                s = iota((rows_tile, block), 1)
                after = position(p, t) > position(p, s)
                same = t == s
                scores = jnp.where(same, 0.0, jnp.where(after, ahead, behind))
                for o, v in enumerate((ahead, behind)):
                    found = jnp.sum(jnp.where(same, v, 0.0), axis=0, keepdims=True)
                    diagonals[o] = diagonals[o] + found

                def weights(h):
                    f = p * 2 * heads + h
                    g = f + heads
                    lead = target[t0 : t0 + rows_tile, f : f + 1] - source[f : f + 1, :]
                    back = target[t0 : t0 + rows_tile, g : g + 1] - source[g : g + 1, :]
                    return (scores * jnp.exp2(jnp.where(after, lead, back))).astype(BF)

                for j in range(heads // 2):
                    pair = jnp.concatenate([weights(2 * j), weights(2 * j + 1)], axis=1)
                    own[
                        p,
                        c * block + t0 : c * block + t0 + rows_tile,
                        2 * j * head : 2 * (j + 1) * head,
                    ] = mm(pair, pairs[j])
            diag = jnp.where(behind_group, diagonals[1], diagonals[0]) * steps
            diag = diag.astype(BF).astype(F32) + skips
            own[p, rows, :] += xf * spread(diag, both_sides, 2)

    def scan(p):
        wait_all(functools.partial(s_copy, p))
        e = spreader(p)
        logs = jnp.concatenate(
            [got[p, i, :, inner:].astype(F32)[0:8] for i in range(n)], axis=0
        )
        logs = logs + pltpu.roll(logs, 8 * n - 1, 0) + pltpu.roll(logs, 8 * n - 2, 0)
        pieces = split(jnp.exp(logs[:, 0:groups]), 3).reshape(3, 8 * n, groups)
        fades = sum(mm(pieces[i], e.astype(BF)) for i in range(3))
        entry = jnp.zeros((part, inner), F32)
        ahead = []
        for i in range(n):
            ahead.append(entry)
            entry = fades[8 * i : 8 * i + 1, :inner] * entry + got[p, i, :, 0:inner].astype(F32)[0:part]
        entry = jnp.zeros((part, inner), F32)
        for i in reversed(range(n)):
            pieces = [ahead[i], entry]
            if 2 * part < 16:
                pieces.append(jnp.zeros((16 - 2 * part, inner), F32))
            ent_out[p, i] = jnp.concatenate(pieces, axis=0).astype(BF)
            entry = (
                fades[8 * i : 8 * i + 1, inner:] * entry + got[p, i, :, 0:inner].astype(F32)[part : 2 * part]
            )
        start_all(functools.partial(e_copy, p))
        ent_in[p, pl.ds(me, 1)] = ent_out[p, pl.ds(me, 1)]

    def finish(p):
        wait_all(functools.partial(e_copy, p))
        arrived = [ent_in[p, i].astype(F32) for i in range(n)]
        entries = [[None] * count, [None] * count]
        for o in range(2):
            entry = jnp.concatenate([v[o * part : (o + 1) * part] for v in arrived], axis=0)
            order = range(count) if o == 0 else reversed(range(count))
            for c in order:
                entries[o][c] = entry.astype(BF)
                lanes = slice(o * inner, (o + 1) * inner)
                entry = fade[p, c : c + 1, lanes] * entry + contrib[p, o, c]
        for c in range(count):
            rows = rows_of(c)
            result = own[p, rows, :]
            for o in range(2):
                reader = coup[p, rows, (2 * o + 1) * state : (2 * o + 2) * state]
                carried = mm(reader, entries[o][c])
                result = result + carried * grown[p, rows, o * inner : (o + 1) * inner]
            if p == 0:
                own[p, rows, :] = result
            else:
                result = result.astype(BF)
                for i in range(n):
                    col_out[i, c * span : (c + 1) * span, :] = result[i * span : (i + 1) * span]

    prepare(1)
    @pl.when(me < n - 1)
    def _():
        halo_copy(1, me + 1).wait_recv()
        halo_copy(0, me + 1).wait_send()

    @pl.when(me == n - 1)
    def _():
        halo[1] = jnp.zeros((width, tokens), BF)

    @pl.when(me > 0)
    def _():
        halo_copy(0, me - 1).wait_recv()
        halo_copy(1, me - 1).wait_send()

    @pl.when(me == 0)
    def _():
        halo[0] = jnp.zeros((width, tokens), BF)

    for slot, a in ((0, 0), (1, 2)):
        rim = mm_tn(normed(halo[slot].astype(F32)), in_w_ref[:, :inner]).astype(BF)
        pre[a, 8 : tokens + 8, :] = rim.astype(F32)
    for c in range(tokens // TILE):
        span_rows = slice(c * TILE, (c + 1) * TILE + 16)
        done = depthwise(lambda a, lanes: pre[a, span_rows, lanes], conv_w_ref, conv_b, TILE)
        xs[0, c * TILE : (c + 1) * TILE, :] = done.astype(BF)
    prepare(0)
    scan(1)
    local(1)
    scan(0)
    finish(1)
    start_all(c_copy)
    col_in[pl.ds(me, 1)] = col_out[pl.ds(me, 1)]
    local(0)
    finish(0)
    wait_all(c_copy)
    for c in range(tokens // TILE):
        rows = slice(c * TILE, (c + 1) * TILE)
        per = TILE // band
        col = col_in[c * per : (c + 1) * per].astype(F32).reshape(TILE, inner)
        gated = (own[0, rows, :] + col) * gate[rows, :]
        mean_square = jnp.mean(gated * gated, axis=-1, keepdims=True)
        normy = (gated * lax.rsqrt(mean_square + EPSILON) * out_gain).astype(BF)
        out_ref[0, :, rows] = (
            region_ref[:, rows].astype(F32) + mm_nt(out_w_ref[...], normy)
        ).astype(BF)
    wait_sent(r_copy)
    for p in range(2):
        wait_sent(functools.partial(s_copy, p))
        wait_sent(functools.partial(e_copy, p))
    wait_sent(c_copy)


def body(n, *args):
    region = args[0]
    _, tokens, width = region.shape
    inner = args[11].shape[0]
    groups = args[7].shape[0]
    heads = groups // 4
    state = args[5].shape[1] // 8
    band = tokens // n
    part = state // n
    block = max(TILE, 16 * n)
    count = tokens // block
    fold = TILE // band
    cell_rows = (width // fold + 8 + 15) // 16 * 16
    flat = [v if v.ndim > 1 else v.reshape(1, -1) for v in args]
    for i in (4, 10):
        if args[i].shape[0] % TILE == 0:
            flat[i] = args[i].reshape(-1, TILE)
    flat[0] = jnp.swapaxes(region, 1, 2)
    flat[6] = flat[6].T
    flat[11] = flat[11].T
    ent_rows = max(16, 2 * part)
    dma = pltpu.SemaphoreType.DMA
    vmem = pltpu.VMEM
    flat = [pltpu.with_memory_space_constraint(v, pltpu.HBM) for v in flat]
    out = pl.pallas_call(
        functools.partial(kernel, n, heads, state, block),
        out_shape=jax.ShapeDtypeStruct(flat[0].shape, BF),
        in_specs=[pl.BlockSpec(memory_space=pltpu.HBM)] * len(flat),
        out_specs=pl.BlockSpec(memory_space=pltpu.VMEM),
        scratch_shapes=[
            vmem((width, tokens), BF),
            *[vmem(v.shape, v.dtype) for v in flat[1:]],
            vmem((n, cell_rows, TILE), BF),
            vmem((n, cell_rows, TILE), BF),
            vmem((2, width, tokens), BF),
            vmem((3, tokens + 16, inner), F32),
            vmem((n + 2, band + 16, inner), F32),
            vmem((tokens, inner), F32),
            vmem((2, tokens, inner), BF),
            vmem((2, tokens, 4 * state), BF),
            vmem((2, groups, tokens), F32),
            vmem((2, groups, tokens), F32),
            vmem((2, 2, count, state, inner), F32),
            vmem((2, 8, 2 * inner), F32),
            vmem((2, tokens, 2 * inner), F32),
            vmem((2, tokens, inner), F32),
            vmem((2, n, ent_rows, inner + TILE), BF),
            vmem((2, n, ent_rows, inner + TILE), BF),
            vmem((2, n, ent_rows, inner), BF),
            vmem((2, n, ent_rows, inner), BF),
            vmem((n, band, inner), BF),
            vmem((n, band, inner), BF),
            dma((len(flat),)),
            dma((n,)),
            dma((n,)),
            dma((2,)),
            dma((2,)),
            dma((2, n)),
            dma((2, n)),
            dma((2, n)),
            dma((2, n)),
            dma((n,)),
            dma((n,)),
        ],
        compiler_params=pltpu.CompilerParams(
            collective_id=0, has_side_effects=True, vmem_limit_bytes=40 * 1024 * 1024
        ),
    )(*flat)
    return jnp.swapaxes(out, 1, 2)


def solution(mesh):
    in_specs = (P(("dp", "seq"), None, None),) + (P(),) * 11
    return jax.shard_map(
        functools.partial(body, mesh.shape["seq"]),
        mesh=mesh,
        in_specs=in_specs,
        out_specs=P(("dp", "seq"), None, None),
        check_vma=False,
    )
```

```python
import functools
import math
import jax
import jax.numpy as jnp
from jax import lax
from jax.experimental import pallas as pl
from jax.experimental.pallas import tpu as pltpu
from jax.sharding import PartitionSpec as P

EPSILON = 1e-05
BF = jnp.bfloat16
F32 = jnp.float32
TILE = 128
LOG2E = math.log2(math.e)


def mm(a, b):
    return jnp.dot(a, b, preferred_element_type=F32)


def mm_nt(a, b):
    return lax.dot_general(a, b, (((1,), (1,)), ((), ())), preferred_element_type=F32)


def mm_tn(a, b):
    return lax.dot_general(a, b, (((0,), (0,)), ((), ())), preferred_element_type=F32)


def split(v, count):
    pieces = []
    for _ in range(count):
        piece = v.astype(BF).astype(F32)
        pieces.append(piece)
        v = v - piece
    return jnp.concatenate(pieces, axis=0).astype(BF)


def iota(shape, dim):
    return lax.broadcasted_iota(jnp.int32, shape, dim)


def silu(v):
    half = 0.5 * v
    return half * jnp.tanh(half) + half


def depthwise(load, weights, bias, size):
    parts = []
    for q in range(weights.shape[1] // TILE):
        lanes = slice(q * TILE, (q + 1) * TILE)
        planes = [load(a, lanes) for a in range(3)]
        sums = []
        for b, first, last in ((0, 0, size + 8), (1, 8, size + 8), (2, 8, size + 16)):
            total = planes[0][first:last] * weights[b : b + 1, lanes]
            for a in (1, 2):
                tap = 3 * a + b
                total = total + planes[a][first:last] * weights[tap : tap + 1, lanes]
            sums.append(total)
        left = pltpu.roll(sums[0], 1, 0)[8:]
        right = pltpu.roll(sums[2], size + 7, 0)[:size]
        parts.append(silu(sums[1] + bias[:, lanes] + (left + right)))
    return jnp.concatenate(parts, axis=1)


def bits(v):
    return v.bit_length() - 1


def one_row(ref):
    return jnp.concatenate([ref[i : i + 1, :] for i in range(ref.shape[0])], axis=1)


def roll_lanes(v, shift):
    shift = shift % v.shape[1]
    return v if shift == 0 else pltpu.roll(v, shift, 1)


def kernel(
    n,
    heads,
    state,
    block,
    region_hbm,
    norm_gain_hbm,
    in_w_hbm,
    conv_w_hbm,
    conv_b_hbm,
    coup_w_hbm,
    step_w_hbm,
    step_b_hbm,
    decay_hbm,
    skip_hbm,
    out_gain_hbm,
    out_w_hbm,
    out_ref,
    region_ref,
    norm_gain_ref,
    in_w_ref,
    conv_w_ref,
    conv_b_ref,
    coup_w_ref,
    step_w_ref,
    step_b_ref,
    decay_ref,
    skip_ref,
    out_gain_ref,
    out_w_ref,
    cells,
    got_cells,
    halo,
    pre,
    pcol,
    gate,
    xs,
    coup,
    cum,
    step_t,
    contrib,
    fade,
    grown,
    own,
    msg,
    got,
    ent_out,
    ent_in,
    col_out,
    col_in,
    local_sem,
    r_send,
    r_recv,
    halo_send,
    halo_recv,
    s_send,
    s_recv,
    e_send,
    e_recv,
    c_send,
    c_recv,
):
    me = lax.axis_index("seq")
    width, tokens = region_ref.shape
    inner = out_w_ref.shape[1]
    band = tokens // n
    head = inner // heads
    part = state // n
    groups = 4 * heads
    count = tokens // block
    span = block // n
    fold = TILE // band
    slab = width // fold
    edge_row = slab

    ring = [(k, lax.rem(me + k, n), lax.rem(me + n - k, n)) for k in range(1, n)]

    barrier = pltpu.get_barrier_semaphore()

    for _, peer, _ in ring:
        pl.semaphore_signal(barrier, inc=1, device_id={"seq": peer})

    sources = (
        region_hbm.at[0],
        norm_gain_hbm,
        in_w_hbm,
        conv_w_hbm,
        conv_b_hbm,
        coup_w_hbm,
        step_w_hbm,
        step_b_hbm,
        decay_hbm,
        skip_hbm,
        out_gain_hbm,
        out_w_hbm,
    )
    targets = (
        region_ref,
        norm_gain_ref,
        in_w_ref,
        conv_w_ref,
        conv_b_ref,
        coup_w_ref,
        step_w_ref,
        step_b_ref,
        decay_ref,
        skip_ref,
        out_gain_ref,
        out_w_ref,
    )
    fetch = [
        pltpu.make_async_copy(source, target, local_sem.at[i])
        for i, (source, target) in enumerate(zip(sources, targets))
    ]
    for copy in fetch:
        copy.start()

    def r_copy(k, chunk, place):
        return pltpu.make_async_remote_copy(
            src_ref=cells.at[chunk],
            dst_ref=got_cells.at[place],
            send_sem=r_send.at[k],
            recv_sem=r_recv.at[k],
            device_id={"seq": chunk},
        )

    def halo_copy(slot, device):
        return pltpu.make_async_remote_copy(
            src_ref=region_ref,
            dst_ref=halo.at[slot],
            send_sem=halo_send.at[slot],
            recv_sem=halo_recv.at[slot],
            device_id={"seq": device},
        )

    def s_copy(p, k, chunk, place):
        return pltpu.make_async_remote_copy(
            src_ref=msg.at[p, chunk],
            dst_ref=got.at[p, place],
            send_sem=s_send.at[p, k],
            recv_sem=s_recv.at[p, k],
            device_id={"seq": chunk},
        )

    def e_copy(p, k, chunk, place):
        return pltpu.make_async_remote_copy(
            src_ref=ent_out.at[p, chunk],
            dst_ref=ent_in.at[p, place],
            send_sem=e_send.at[p, k],
            recv_sem=e_recv.at[p, k],
            device_id={"seq": chunk},
        )

    def c_copy(k, chunk, place):
        return pltpu.make_async_remote_copy(
            src_ref=col_out.at[chunk],
            dst_ref=col_in.at[place],
            send_sem=c_send.at[k],
            recv_sem=c_recv.at[k],
            device_id={"seq": chunk},
        )

    def start_all(make, partners=ring):
        for k, peer, _ in partners:
            make(k, peer, me).start()

    def wait_all(make, partners=ring):
        for k, peer, source in partners:
            make(k, peer, source).wait_recv()

    def wait_sent(make, partners=ring):
        for k, peer, source in partners:
            make(k, peer, source).wait_send()

    piece = jnp.right_shift(iota((slab, TILE), 1), bits(band))
    fetch[0].wait()
    rest = cells.shape[1] - slab - 8
    sel_row = iota((8 * n, tokens), 0)
    sel_band = jnp.right_shift(sel_row, 3)
    sel_kind = jnp.bitwise_and(sel_row, 7)
    sel_cell = iota((8 * n, tokens), 1)
    side = jnp.where(
        jnp.bitwise_and(sel_kind, 1) == 0, sel_band * band - 1, sel_band * band + band
    )
    hit = sel_cell == side
    low = jnp.where(hit & (sel_kind < 2), 1.0, 0.0).astype(BF)
    high = jnp.where(hit & (sel_kind >= 2) & (sel_kind < 4), 1.0, 0.0).astype(BF)
    edges = mm_nt(low, region_ref[0:TILE, :]) + mm_nt(high, region_ref[width - TILE : width, :])
    for m in range(tokens // TILE):
        lanes = region_ref[:, m * TILE : (m + 1) * TILE].astype(F32)
        for r in range(fold):
            packed = lanes[0:slab]
            packed = roll_lanes(packed, (0 - r) * band)
            for q in range(1, fold):
                moved = roll_lanes(lanes[q * slab : (q + 1) * slab], (q - r) * band)
                packed = jnp.where(piece == q, moved, packed)
            d = m * fold + r
            parts = [packed, edges[8 * d : 8 * d + 8]]
            if rest:
                parts.append(jnp.zeros((rest, TILE), F32))
            cells[d] = jnp.concatenate(parts, axis=0).astype(BF)

    pl.semaphore_wait(barrier, n - 1)
    start_all(r_copy)

    @pl.when(me < n - 1)
    def _():
        halo_copy(0, me + 1).start()

    @pl.when(me > 0)
    def _():
        halo_copy(1, me - 1).start()

    got_cells[pl.ds(me, 1)] = cells[pl.ds(me, 1)]

    for copy in fetch[1:]:
        copy.wait()
    gain_row = norm_gain_ref[...]
    conv_b = one_row(conv_b_ref)
    out_gain = one_row(out_gain_ref)
    gain_col = jnp.broadcast_to(gain_row, (8, width)).T[:, 0:1]

    def normed(values):
        mean_square = jnp.mean(values * values, axis=0, keepdims=True)
        return (values * lax.rsqrt(mean_square + EPSILON) * gain_col).astype(BF)

    edge = jnp.zeros((8, inner), F32)
    for a in range(3):
        pre[a, 0:8, :] = edge
        pre[a, tokens + 8 : tokens + 16, :] = edge
    blank = jnp.zeros((band + 16, inner), F32)
    pcol[0] = blank
    pcol[n + 1] = blank
    mine = mm_tn(normed(region_ref[...].astype(F32)), in_w_ref[...]).astype(BF)
    pre[1, 8 : tokens + 8, :] = mine[:, :inner].astype(F32)
    gate[...] = silu(mine[:, inner:].astype(F32))

    wait_all(r_copy)

    for m in range(tokens // TILE):
        slabs = []
        for q in range(fold):
            packed = None
            for r in range(fold):
                moved = roll_lanes(
                    got_cells[m * fold + r, 0:slab, :].astype(F32), (r - q) * band
                )
                packed = moved if packed is None else jnp.where(piece == r, moved, packed)
            slabs.append(packed)
        values = normed(jnp.concatenate(slabs, axis=0))
        done = mm_tn(values, in_w_ref[:, :inner]).astype(BF).astype(F32)
        for r in range(fold):
            pcol[m * fold + r + 1, 8 : band + 8, :] = done[r * band : (r + 1) * band]
    rims = jnp.concatenate(
        [got_cells[i, edge_row : cells.shape[1], :].astype(F32)[0:8] for i in range(n)], axis=0
    )
    rim_low = rims
    rim_high = jnp.where(
        iota((8 * n, TILE), 1) >= 2 * TILE - width, pltpu.roll(rims, 8 * n - 2, 0), 0.0
    )
    mean_square = (
        jnp.sum(rim_low * rim_low, axis=-1, keepdims=True)
        + jnp.sum(rim_high * rim_high, axis=-1, keepdims=True)
    ) / width
    scale = lax.rsqrt(mean_square + EPSILON)
    rim_pre = mm(
        (rim_low * scale * gain_row[:, 0:TILE]).astype(BF), in_w_ref[0:TILE, :inner]
    ) + mm(
        (rim_high * scale * gain_row[:, width - TILE : width]).astype(BF),
        in_w_ref[width - TILE : width, :inner],
    )
    rim_pre = rim_pre.astype(BF).astype(F32)
    for i in range(n):
        pcol[i + 1, 7:8, :] = rim_pre[8 * i : 8 * i + 1]
        pcol[i + 1, band + 8 : band + 9, :] = rim_pre[8 * i + 1 : 8 * i + 2]
    for i in range(n):
        done = depthwise(lambda a, lanes: pcol[i + a, :, lanes], conv_w_ref, conv_b, band).astype(BF)
        for c in range(count):
            start = c * block + i * span
            xs[1, start : start + span, :] = done[c * span : (c + 1) * span]

    group = iota((groups, 1), 0)
    behind_group = lax.rem(group, 2 * heads) >= heads
    behind_lane = lax.rem(iota((1, groups), 1), 2 * heads) >= heads
    eye = iota((groups, groups), 0) == iota((groups, groups), 1)

    def column_of(row):
        return jnp.sum(jnp.where(eye, row, 0.0), axis=1, keepdims=True)

    def row_of(column):
        here = iota((groups, TILE), 0) == iota((groups, TILE), 1)
        return jnp.sum(jnp.where(here, column, 0.0), axis=0, keepdims=True)

    rates = -jnp.exp(column_of(decay_ref[...]))
    step_b = column_of(step_b_ref[...])
    skips = column_of(skip_ref[...])

    def spreader(p):
        where = jnp.right_shift(iota((groups, 2 * inner), 1), bits(head))
        return (iota((groups, 2 * inner), 0) == where + p * 2 * heads).astype(F32)

    def spread(v, e, pieces):
        many = jnp.concatenate([e] * pieces, axis=0).astype(BF)
        return mm_tn(split(v, pieces), many)

    def position(p, v):
        if p == 0:
            return v
        return jnp.bitwise_and(v, span - 1) * n + jnp.right_shift(v, bits(span))

    def rows_of(c):
        return slice(c * block, (c + 1) * block)

    def prepare(p):
        x = xs[p]
        first = p * 4 * state
        coup[p] = mm(x, coup_w_ref[:, first : first + 4 * state]).astype(BF)
        logits = mm_nt(step_w_ref[...], x) + step_b
        steps = jnp.maximum(logits, 0.0) + jnp.log1p(jnp.exp(-jnp.abs(logits)))
        logs = rates * steps
        step_t[p] = steps
        pieces = split(logs, 3)
        earlier = position(p, iota((block, block), 0)) <= position(p, iota((block, block), 1))
        earlier = jnp.where(earlier, 1.0, 0.0).astype(BF)
        e = spreader(p)
        lane = iota((groups, TILE), 1)
        totals = jnp.zeros((groups, TILE), F32)
        whole = jnp.zeros((groups, 1), F32)
        for c in range(count):
            rows = rows_of(c)
            sums = mm(pieces[:, rows], earlier)
            ahead = sums[0:groups] + sums[groups : 2 * groups] + sums[2 * groups : 3 * groups]
            total = ahead[:, block - 1 : block]
            level = jnp.where(behind_group, total - ahead + logs[:, rows], ahead)
            cum[p, :, rows] = level
            totals = jnp.where(lane == c, total, totals)
            whole = whole + total
            tails = spread(jnp.exp(total - level) * steps[:, rows], e, 2)
            xf = xs[p, rows, :].astype(F32)
            for o in range(2):
                weighted = (xf * tails[:, o * inner : (o + 1) * inner]).astype(BF)
                writer = coup[p, rows, 2 * o * state : (2 * o + 1) * state]
                contrib[p, o, c] = mm_tn(writer, weighted)
        left = row_of(whole)
        line = iota((msg.shape[2], TILE), 0)
        totals_sent = jnp.zeros((msg.shape[2], TILE), F32)
        for i in range(3):
            rounded = left.astype(BF).astype(F32)
            totals_sent = jnp.where(line == i, rounded, totals_sent)
            left = left - rounded
        totals_sent = totals_sent.astype(BF)
        fade[p] = spread(jnp.exp(totals), e, 3)[0:8]
        sums = [contrib[p, 0, 0], contrib[p, 1, count - 1]]
        for c in range(1, count):
            sums[0] = fade[p, c : c + 1, :inner] * sums[0] + contrib[p, 0, c]
            back = count - 1 - c
            sums[1] = fade[p, back : back + 1, inner:] * sums[1] + contrib[p, 1, back]
        for d in range(n):
            pieces = [v[d * part : (d + 1) * part] for v in sums]
            if 2 * part < 16:
                pieces.append(jnp.zeros((16 - 2 * part, inner), F32))
            msg[p, d, :, 0:inner] = jnp.concatenate(pieces, axis=0).astype(BF)
            msg[p, d, :, inner:] = totals_sent
        start_all(functools.partial(s_copy, p))
        got[p, pl.ds(me, 1)] = msg[p, pl.ds(me, 1)]

    def prepare_stacked(p):
        x = xs[p]
        first = p * 4 * state
        coup[p] = mm(x, coup_w_ref[:, first : first + 4 * state]).astype(BF)
        logits = mm_nt(step_w_ref[...], x) + step_b
        steps = jnp.maximum(logits, 0.0) + jnp.log1p(jnp.exp(-jnp.abs(logits)))
        logs = rates * steps
        step_t[p] = steps
        earlier = position(p, iota((block, block), 0)) <= position(p, iota((block, block), 1))
        earlier = jnp.where(earlier, 1.0, 0.0).astype(BF)

        def stack(v):
            return jnp.concatenate([v[:, rows_of(c)] for c in range(count)], axis=0)

        deep = count * groups
        behind_deep = lax.rem(iota((deep, 1), 0), 2 * heads) >= heads
        stacked = stack(logs)
        sums = mm(split(stacked, 3), earlier)
        ahead = sums[0:deep] + sums[deep : 2 * deep] + sums[2 * deep : 3 * deep]
        total = ahead[:, block - 1 : block]
        level = jnp.where(behind_deep, total - ahead + stacked, ahead)
        tail = jnp.exp(total - level) * stack(steps)
        e = spreader(p)
        lane = iota((groups, TILE), 1)
        totals = jnp.zeros((groups, TILE), F32)
        whole = jnp.zeros((groups, 1), F32)
        for c in range(count):
            rows = rows_of(c)
            these = slice(c * groups, (c + 1) * groups)
            cum[p, :, rows] = level[these]
            totals = jnp.where(lane == c, total[these], totals)
            whole = whole + total[these]
            tails = spread(tail[these], e, 2)
            xf = xs[p, rows, :].astype(F32)
            for o in range(2):
                weighted = (xf * tails[:, o * inner : (o + 1) * inner]).astype(BF)
                writer = coup[p, rows, 2 * o * state : (2 * o + 1) * state]
                contrib[p, o, c] = mm_tn(writer, weighted)
        left = row_of(whole)
        line = iota((msg.shape[2], TILE), 0)
        totals_sent = jnp.zeros((msg.shape[2], TILE), F32)
        for i in range(3):
            rounded = left.astype(BF).astype(F32)
            totals_sent = jnp.where(line == i, rounded, totals_sent)
            left = left - rounded
        totals_sent = totals_sent.astype(BF)
        fade[p] = spread(jnp.exp(totals), e, 3)[0:8]
        sums = [contrib[p, 0, 0], contrib[p, 1, count - 1]]
        for c in range(1, count):
            sums[0] = fade[p, c : c + 1, :inner] * sums[0] + contrib[p, 0, c]
            back = count - 1 - c
            sums[1] = fade[p, back : back + 1, inner:] * sums[1] + contrib[p, 1, back]
        for d in range(n):
            pieces = [v[d * part : (d + 1) * part] for v in sums]
            if 2 * part < 16:
                pieces.append(jnp.zeros((16 - 2 * part, inner), F32))
            msg[p, d, :, 0:inner] = jnp.concatenate(pieces, axis=0).astype(BF)
            msg[p, d, :, inner:] = totals_sent
        start_all(functools.partial(s_copy, p))
        got[p, pl.ds(me, 1)] = msg[p, pl.ds(me, 1)]

    def local(p):
        e = spreader(p)
        both_sides = e[:, :inner] + e[:, inner:]
        eyes = eye.astype(F32)
        rows_tile = min(block, TILE)
        even = jnp.bitwise_and(iota((1, 2 * head), 1), head) == 0
        for c in range(count):
            rows = rows_of(c)
            level = cum[p, :, rows]
            steps = step_t[p, :, rows]
            grown[p, rows, :] = spread(jnp.exp(level), e, 2)
            scaled = level * LOG2E
            source = scaled - jnp.log(steps) * LOG2E
            target = spread(scaled, eyes, 3)
            xf = xs[p, rows, :].astype(F32)
            pairs = []
            for j in range(heads // 2):
                lanes = xf[:, 2 * j * head : 2 * (j + 1) * head]
                pairs.append(
                    jnp.concatenate(
                        [jnp.where(even, lanes, 0.0), jnp.where(even, 0.0, lanes)], axis=0
                    ).astype(BF)
                )
            diagonals = [jnp.zeros((1, block), F32)] * 2
            for q in range(block // rows_tile):
                t0 = q * rows_tile
                mine = coup[p, c * block + t0 : c * block + t0 + rows_tile, :]
                ahead = mm_nt(mine[:, state : 2 * state], coup[p, rows, 0:state])
                behind = mm_nt(mine[:, 3 * state :], coup[p, rows, 2 * state : 3 * state])
                t = iota((rows_tile, block), 0) + t0
                s = iota((rows_tile, block), 1)
                after = position(p, t) > position(p, s)
                same = t == s
                scores = jnp.where(same, 0.0, jnp.where(after, ahead, behind))
                for o, v in enumerate((ahead, behind)):
                    found = jnp.sum(jnp.where(same, v, 0.0), axis=0, keepdims=True)
                    diagonals[o] = diagonals[o] + found

                def weights(h):
                    f = p * 2 * heads + h
                    g = f + heads
                    lead = target[t0 : t0 + rows_tile, f : f + 1] - source[f : f + 1, :]
                    back = target[t0 : t0 + rows_tile, g : g + 1] - source[g : g + 1, :]
                    return (scores * jnp.exp2(jnp.where(after, lead, back))).astype(BF)

                for j in range(heads // 2):
                    pair = jnp.concatenate([weights(2 * j), weights(2 * j + 1)], axis=1)
                    own[
                        p,
                        c * block + t0 : c * block + t0 + rows_tile,
                        2 * j * head : 2 * (j + 1) * head,
                    ] = mm(pair, pairs[j])
            diag = jnp.where(behind_group, diagonals[1], diagonals[0]) * steps
            diag = diag.astype(BF).astype(F32) + skips
            own[p, rows, :] += xf * spread(diag, both_sides, 2)

    def scan(p):
        wait_all(functools.partial(s_copy, p))
        e = spreader(p)
        logs = jnp.concatenate(
            [got[p, i, :, inner:].astype(F32)[0:8] for i in range(n)], axis=0
        )
        logs = logs + pltpu.roll(logs, 8 * n - 1, 0) + pltpu.roll(logs, 8 * n - 2, 0)
        pieces = split(jnp.exp(logs[:, 0:groups]), 3).reshape(3, 8 * n, groups)
        fades = sum(mm(pieces[i], e.astype(BF)) for i in range(3))
        entry = jnp.zeros((part, inner), F32)
        ahead = []
        for i in range(n):
            ahead.append(entry)
            entry = fades[8 * i : 8 * i + 1, :inner] * entry + got[p, i, :, 0:inner].astype(F32)[0:part]
        entry = jnp.zeros((part, inner), F32)
        for i in reversed(range(n)):
            pieces = [ahead[i], entry]
            if 2 * part < 16:
                pieces.append(jnp.zeros((16 - 2 * part, inner), F32))
            ent_out[p, i] = jnp.concatenate(pieces, axis=0).astype(BF)
            entry = (
                fades[8 * i : 8 * i + 1, inner:] * entry + got[p, i, :, 0:inner].astype(F32)[part : 2 * part]
            )
        start_all(functools.partial(e_copy, p))
        ent_in[p, pl.ds(me, 1)] = ent_out[p, pl.ds(me, 1)]

    def finish(p):
        wait_all(functools.partial(e_copy, p))
        arrived = [ent_in[p, i].astype(F32) for i in range(n)]
        entries = [[None] * count, [None] * count]
        for o in range(2):
            entry = jnp.concatenate([v[o * part : (o + 1) * part] for v in arrived], axis=0)
            order = range(count) if o == 0 else reversed(range(count))
            for c in order:
                entries[o][c] = entry.astype(BF)
                lanes = slice(o * inner, (o + 1) * inner)
                entry = fade[p, c : c + 1, lanes] * entry + contrib[p, o, c]
        for c in range(count):
            rows = rows_of(c)
            result = own[p, rows, :]
            for o in range(2):
                reader = coup[p, rows, (2 * o + 1) * state : (2 * o + 2) * state]
                carried = mm(reader, entries[o][c])
                result = result + carried * grown[p, rows, o * inner : (o + 1) * inner]
            if p == 0:
                own[p, rows, :] = result
            else:
                result = result.astype(BF)
                for i in range(n):
                    col_out[i, c * span : (c + 1) * span, :] = result[i * span : (i + 1) * span]

    prepare(1)
    @pl.when(me < n - 1)
    def _():
        halo_copy(1, me + 1).wait_recv()
        halo_copy(0, me + 1).wait_send()

    @pl.when(me == n - 1)
    def _():
        halo[1] = jnp.zeros((width, tokens), BF)

    @pl.when(me > 0)
    def _():
        halo_copy(0, me - 1).wait_recv()
        halo_copy(1, me - 1).wait_send()

    @pl.when(me == 0)
    def _():
        halo[0] = jnp.zeros((width, tokens), BF)

    for slot, a in ((0, 0), (1, 2)):
        rim = mm_tn(normed(halo[slot].astype(F32)), in_w_ref[:, :inner]).astype(BF)
        pre[a, 8 : tokens + 8, :] = rim.astype(F32)
    for c in range(tokens // TILE):
        span_rows = slice(c * TILE, (c + 1) * TILE + 16)
        done = depthwise(lambda a, lanes: pre[a, span_rows, lanes], conv_w_ref, conv_b, TILE)
        xs[0, c * TILE : (c + 1) * TILE, :] = done.astype(BF)
    prepare_stacked(0)
    scan(1)
    local(1)
    scan(0)
    finish(1)
    start_all(c_copy)
    col_in[pl.ds(me, 1)] = col_out[pl.ds(me, 1)]
    local(0)
    finish(0)
    wait_all(c_copy)
    for c in range(tokens // TILE):
        rows = slice(c * TILE, (c + 1) * TILE)
        per = TILE // band
        col = col_in[c * per : (c + 1) * per].astype(F32).reshape(TILE, inner)
        gated = (own[0, rows, :] + col) * gate[rows, :]
        mean_square = jnp.mean(gated * gated, axis=-1, keepdims=True)
        normy = (gated * lax.rsqrt(mean_square + EPSILON) * out_gain).astype(BF)
        out_ref[0, :, rows] = (
            region_ref[:, rows].astype(F32) + mm_nt(out_w_ref[...], normy)
        ).astype(BF)
    wait_sent(r_copy)
    for p in range(2):
        wait_sent(functools.partial(s_copy, p))
        wait_sent(functools.partial(e_copy, p))
    wait_sent(c_copy)


def body(n, *args):
    region = args[0]
    _, tokens, width = region.shape
    inner = args[11].shape[0]
    groups = args[7].shape[0]
    heads = groups // 4
    state = args[5].shape[1] // 8
    band = tokens // n
    part = state // n
    block = max(TILE, 16 * n)
    count = tokens // block
    fold = TILE // band
    cell_rows = (width // fold + 8 + 15) // 16 * 16
    flat = [v if v.ndim > 1 else v.reshape(1, -1) for v in args]
    for i in (4, 10):
        if args[i].shape[0] % TILE == 0:
            flat[i] = args[i].reshape(-1, TILE)
    flat[0] = jnp.swapaxes(region, 1, 2)
    flat[6] = flat[6].T
    flat[11] = flat[11].T
    ent_rows = max(16, 2 * part)
    dma = pltpu.SemaphoreType.DMA
    vmem = pltpu.VMEM
    flat = [pltpu.with_memory_space_constraint(v, pltpu.HBM) for v in flat]
    out = pl.pallas_call(
        functools.partial(kernel, n, heads, state, block),
        out_shape=jax.ShapeDtypeStruct(flat[0].shape, BF),
        in_specs=[pl.BlockSpec(memory_space=pltpu.HBM)] * len(flat),
        out_specs=pl.BlockSpec(memory_space=pltpu.VMEM),
        scratch_shapes=[
            vmem((width, tokens), BF),
            *[vmem(v.shape, v.dtype) for v in flat[1:]],
            vmem((n, cell_rows, TILE), BF),
            vmem((n, cell_rows, TILE), BF),
            vmem((2, width, tokens), BF),
            vmem((3, tokens + 16, inner), F32),
            vmem((n + 2, band + 16, inner), F32),
            vmem((tokens, inner), F32),
            vmem((2, tokens, inner), BF),
            vmem((2, tokens, 4 * state), BF),
            vmem((2, groups, tokens), F32),
            vmem((2, groups, tokens), F32),
            vmem((2, 2, count, state, inner), F32),
            vmem((2, 8, 2 * inner), F32),
            vmem((2, tokens, 2 * inner), F32),
            vmem((2, tokens, inner), F32),
            vmem((2, n, ent_rows, inner + TILE), BF),
            vmem((2, n, ent_rows, inner + TILE), BF),
            vmem((2, n, ent_rows, inner), BF),
            vmem((2, n, ent_rows, inner), BF),
            vmem((n, band, inner), BF),
            vmem((n, band, inner), BF),
            dma((len(flat),)),
            dma((n,)),
            dma((n,)),
            dma((2,)),
            dma((2,)),
            dma((2, n)),
            dma((2, n)),
            dma((2, n)),
            dma((2, n)),
            dma((n,)),
            dma((n,)),
        ],
        compiler_params=pltpu.CompilerParams(
            collective_id=0, has_side_effects=True, vmem_limit_bytes=40 * 1024 * 1024
        ),
    )(*flat)
    return jnp.swapaxes(out, 1, 2)


def solution(mesh):
    in_specs = (P(("dp", "seq"), None, None),) + (P(),) * 11
    return jax.shard_map(
        functools.partial(body, mesh.shape["seq"]),
        mesh=mesh,
        in_specs=in_specs,
        out_specs=P(("dp", "seq"), None, None),
        check_vma=False,
    )
```

```python
import functools
import math
import jax
import jax.numpy as jnp
from jax import lax
from jax.experimental import pallas as pl
from jax.experimental.pallas import tpu as pltpu
from jax.sharding import PartitionSpec as P

EPSILON = 1e-05
BF = jnp.bfloat16
F32 = jnp.float32
TILE = 128
LOG2E = math.log2(math.e)


def mm(a, b):
    return jnp.dot(a, b, preferred_element_type=F32)


def mm_nt(a, b):
    return lax.dot_general(a, b, (((1,), (1,)), ((), ())), preferred_element_type=F32)


def mm_tn(a, b):
    return lax.dot_general(a, b, (((0,), (0,)), ((), ())), preferred_element_type=F32)


def split(v, count):
    pieces = []
    for _ in range(count):
        piece = v.astype(BF).astype(F32)
        pieces.append(piece)
        v = v - piece
    return jnp.concatenate(pieces, axis=0).astype(BF)


def iota(shape, dim):
    return lax.broadcasted_iota(jnp.int32, shape, dim)


def silu(v):
    half = 0.5 * v
    return half * jnp.tanh(half) + half


def depthwise(load, weights, bias, size):
    parts = []
    for q in range(weights.shape[1] // TILE):
        lanes = slice(q * TILE, (q + 1) * TILE)
        planes = [load(a, lanes) for a in range(3)]
        sums = []
        for b, first, last in ((0, 0, size + 8), (1, 8, size + 8), (2, 8, size + 16)):
            total = planes[0][first:last] * weights[b : b + 1, lanes]
            for a in (1, 2):
                tap = 3 * a + b
                total = total + planes[a][first:last] * weights[tap : tap + 1, lanes]
            sums.append(total)
        left = pltpu.roll(sums[0], 1, 0)[8:]
        right = pltpu.roll(sums[2], size + 7, 0)[:size]
        parts.append(silu(sums[1] + bias[:, lanes] + (left + right)))
    return jnp.concatenate(parts, axis=1)


def bits(v):
    return v.bit_length() - 1


def one_row(ref):
    return jnp.concatenate([ref[i : i + 1, :] for i in range(ref.shape[0])], axis=1)


def roll_lanes(v, shift):
    shift = shift % v.shape[1]
    return v if shift == 0 else pltpu.roll(v, shift, 1)


def kernel(
    n,
    heads,
    state,
    block,
    region_hbm,
    norm_gain_hbm,
    in_w_hbm,
    conv_w_hbm,
    conv_b_hbm,
    coup_w_hbm,
    step_w_hbm,
    step_b_hbm,
    decay_hbm,
    skip_hbm,
    out_gain_hbm,
    out_w_hbm,
    out_ref,
    region_ref,
    norm_gain_ref,
    in_w_ref,
    conv_w_ref,
    conv_b_ref,
    coup_w_ref,
    step_w_ref,
    step_b_ref,
    decay_ref,
    skip_ref,
    out_gain_ref,
    out_w_ref,
    cells,
    got_cells,
    halo,
    pre,
    pcol,
    gate,
    xs,
    coup,
    cum,
    step_t,
    contrib,
    fade,
    grown,
    own,
    msg,
    got,
    ent_out,
    ent_in,
    col_out,
    col_in,
    local_sem,
    r_send,
    r_recv,
    halo_send,
    halo_recv,
    s_send,
    s_recv,
    e_send,
    e_recv,
    c_send,
    c_recv,
):
    me = lax.axis_index("seq")
    width, tokens = region_ref.shape
    inner = out_w_ref.shape[1]
    band = tokens // n
    head = inner // heads
    part = state // n
    groups = 4 * heads
    count = tokens // block
    span = block // n
    fold = TILE // band
    slab = width // fold
    edge_row = slab

    ring = [(k, lax.rem(me + k, n), lax.rem(me + n - k, n)) for k in range(1, n)]

    barrier = pltpu.get_barrier_semaphore()

    for _, peer, _ in ring:
        pl.semaphore_signal(barrier, inc=1, device_id={"seq": peer})

    sources = (
        region_hbm.at[0],
        norm_gain_hbm,
        in_w_hbm,
        conv_w_hbm,
        conv_b_hbm,
        coup_w_hbm,
        step_w_hbm,
        step_b_hbm,
        decay_hbm,
        skip_hbm,
        out_gain_hbm,
        out_w_hbm,
    )
    targets = (
        region_ref,
        norm_gain_ref,
        in_w_ref,
        conv_w_ref,
        conv_b_ref,
        coup_w_ref,
        step_w_ref,
        step_b_ref,
        decay_ref,
        skip_ref,
        out_gain_ref,
        out_w_ref,
    )
    fetch = [
        pltpu.make_async_copy(source, target, local_sem.at[i])
        for i, (source, target) in enumerate(zip(sources, targets))
    ]
    for copy in fetch:
        copy.start()

    def r_copy(k, chunk, place):
        return pltpu.make_async_remote_copy(
            src_ref=cells.at[chunk],
            dst_ref=got_cells.at[place],
            send_sem=r_send.at[k],
            recv_sem=r_recv.at[k],
            device_id={"seq": chunk},
        )

    def halo_copy(slot, device):
        return pltpu.make_async_remote_copy(
            src_ref=region_ref,
            dst_ref=halo.at[slot],
            send_sem=halo_send.at[slot],
            recv_sem=halo_recv.at[slot],
            device_id={"seq": device},
        )

    def s_copy(p, k, chunk, place):
        return pltpu.make_async_remote_copy(
            src_ref=msg.at[p, chunk],
            dst_ref=got.at[p, place],
            send_sem=s_send.at[p, k],
            recv_sem=s_recv.at[p, k],
            device_id={"seq": chunk},
        )

    def e_copy(p, k, chunk, place):
        return pltpu.make_async_remote_copy(
            src_ref=ent_out.at[p, chunk],
            dst_ref=ent_in.at[p, place],
            send_sem=e_send.at[p, k],
            recv_sem=e_recv.at[p, k],
            device_id={"seq": chunk},
        )

    def c_copy(k, chunk, place):
        return pltpu.make_async_remote_copy(
            src_ref=col_out.at[chunk],
            dst_ref=col_in.at[place],
            send_sem=c_send.at[k],
            recv_sem=c_recv.at[k],
            device_id={"seq": chunk},
        )

    def start_all(make, partners=ring):
        for k, peer, _ in partners:
            make(k, peer, me).start()

    def wait_all(make, partners=ring):
        for k, peer, source in partners:
            make(k, peer, source).wait_recv()

    def wait_sent(make, partners=ring):
        for k, peer, source in partners:
            make(k, peer, source).wait_send()

    piece = jnp.right_shift(iota((slab, TILE), 1), bits(band))
    fetch[0].wait()
    rest = cells.shape[1] - slab - 8
    sel_row = iota((8 * n, tokens), 0)
    sel_band = jnp.right_shift(sel_row, 3)
    sel_kind = jnp.bitwise_and(sel_row, 7)
    sel_cell = iota((8 * n, tokens), 1)
    side = jnp.where(
        jnp.bitwise_and(sel_kind, 1) == 0, sel_band * band - 1, sel_band * band + band
    )
    hit = sel_cell == side
    low = jnp.where(hit & (sel_kind < 2), 1.0, 0.0).astype(BF)
    high = jnp.where(hit & (sel_kind >= 2) & (sel_kind < 4), 1.0, 0.0).astype(BF)
    edges = mm_nt(low, region_ref[0:TILE, :]) + mm_nt(high, region_ref[width - TILE : width, :])
    for m in range(tokens // TILE):
        lanes = region_ref[:, m * TILE : (m + 1) * TILE].astype(F32)
        for r in range(fold):
            packed = lanes[0:slab]
            packed = roll_lanes(packed, (0 - r) * band)
            for q in range(1, fold):
                moved = roll_lanes(lanes[q * slab : (q + 1) * slab], (q - r) * band)
                packed = jnp.where(piece == q, moved, packed)
            d = m * fold + r
            parts = [packed, edges[8 * d : 8 * d + 8]]
            if rest:
                parts.append(jnp.zeros((rest, TILE), F32))
            cells[d] = jnp.concatenate(parts, axis=0).astype(BF)

    pl.semaphore_wait(barrier, n - 1)
    start_all(r_copy)

    @pl.when(me < n - 1)
    def _():
        halo_copy(0, me + 1).start()

    @pl.when(me > 0)
    def _():
        halo_copy(1, me - 1).start()

    got_cells[pl.ds(me, 1)] = cells[pl.ds(me, 1)]

    for copy in fetch[1:]:
        copy.wait()
    gain_row = norm_gain_ref[...]
    conv_b = one_row(conv_b_ref)
    out_gain = one_row(out_gain_ref)
    gain_col = jnp.broadcast_to(gain_row, (8, width)).T[:, 0:1]

    def normed(values):
        mean_square = jnp.mean(values * values, axis=0, keepdims=True)
        return (values * lax.rsqrt(mean_square + EPSILON) * gain_col).astype(BF)

    edge = jnp.zeros((8, inner), F32)
    for a in range(3):
        pre[a, 0:8, :] = edge
        pre[a, tokens + 8 : tokens + 16, :] = edge
    blank = jnp.zeros((band + 16, inner), F32)
    pcol[0] = blank
    pcol[n + 1] = blank
    mine = mm_tn(normed(region_ref[...].astype(F32)), in_w_ref[...]).astype(BF)
    pre[1, 8 : tokens + 8, :] = mine[:, :inner].astype(F32)
    gate[...] = silu(mine[:, inner:].astype(F32))

    wait_all(r_copy)

    for m in range(tokens // TILE):
        slabs = []
        for q in range(fold):
            packed = None
            for r in range(fold):
                moved = roll_lanes(
                    got_cells[m * fold + r, 0:slab, :].astype(F32), (r - q) * band
                )
                packed = moved if packed is None else jnp.where(piece == r, moved, packed)
            slabs.append(packed)
        values = normed(jnp.concatenate(slabs, axis=0))
        done = mm_tn(values, in_w_ref[:, :inner]).astype(BF).astype(F32)
        for r in range(fold):
            pcol[m * fold + r + 1, 8 : band + 8, :] = done[r * band : (r + 1) * band]
    rims = jnp.concatenate(
        [got_cells[i, edge_row : cells.shape[1], :].astype(F32)[0:8] for i in range(n)], axis=0
    )
    rim_low = rims
    rim_high = jnp.where(
        iota((8 * n, TILE), 1) >= 2 * TILE - width, pltpu.roll(rims, 8 * n - 2, 0), 0.0
    )
    mean_square = (
        jnp.sum(rim_low * rim_low, axis=-1, keepdims=True)
        + jnp.sum(rim_high * rim_high, axis=-1, keepdims=True)
    ) / width
    scale = lax.rsqrt(mean_square + EPSILON)
    rim_pre = mm(
        (rim_low * scale * gain_row[:, 0:TILE]).astype(BF), in_w_ref[0:TILE, :inner]
    ) + mm(
        (rim_high * scale * gain_row[:, width - TILE : width]).astype(BF),
        in_w_ref[width - TILE : width, :inner],
    )
    rim_pre = rim_pre.astype(BF).astype(F32)
    for i in range(n):
        pcol[i + 1, 7:8, :] = rim_pre[8 * i : 8 * i + 1]
        pcol[i + 1, band + 8 : band + 9, :] = rim_pre[8 * i + 1 : 8 * i + 2]
    for i in range(n):
        done = depthwise(lambda a, lanes: pcol[i + a, :, lanes], conv_w_ref, conv_b, band).astype(BF)
        for c in range(count):
            start = c * block + i * span
            xs[1, start : start + span, :] = done[c * span : (c + 1) * span]

    group = iota((groups, 1), 0)
    behind_group = lax.rem(group, 2 * heads) >= heads
    behind_lane = lax.rem(iota((1, groups), 1), 2 * heads) >= heads
    eye = iota((groups, groups), 0) == iota((groups, groups), 1)

    def column_of(row):
        return jnp.sum(jnp.where(eye, row, 0.0), axis=1, keepdims=True)

    def row_of(column):
        here = iota((groups, TILE), 0) == iota((groups, TILE), 1)
        return jnp.sum(jnp.where(here, column, 0.0), axis=0, keepdims=True)

    rates = -jnp.exp(column_of(decay_ref[...]))
    step_b = column_of(step_b_ref[...])
    skips = column_of(skip_ref[...])

    def spreader(p):
        where = jnp.right_shift(iota((groups, 2 * inner), 1), bits(head))
        return (iota((groups, 2 * inner), 0) == where + p * 2 * heads).astype(F32)

    def spread(v, e, pieces):
        many = jnp.concatenate([e] * pieces, axis=0).astype(BF)
        return mm_tn(split(v, pieces), many)

    def position(p, v):
        if p == 0:
            return v
        return jnp.bitwise_and(v, span - 1) * n + jnp.right_shift(v, bits(span))

    def rows_of(c):
        return slice(c * block, (c + 1) * block)

    def prepare(p):
        x = xs[p]
        first = p * 4 * state
        coup[p] = mm(x, coup_w_ref[:, first : first + 4 * state]).astype(BF)
        logits = mm_nt(step_w_ref[...], x) + step_b
        steps = jnp.maximum(logits, 0.0) + jnp.log1p(jnp.exp(-jnp.abs(logits)))
        logs = rates * steps
        step_t[p] = steps
        pieces = split(logs, 3)
        earlier = position(p, iota((block, block), 0)) <= position(p, iota((block, block), 1))
        earlier = jnp.where(earlier, 1.0, 0.0).astype(BF)
        e = spreader(p)
        lane = iota((groups, TILE), 1)
        totals = jnp.zeros((groups, TILE), F32)
        whole = jnp.zeros((groups, 1), F32)
        for c in range(count):
            rows = rows_of(c)
            sums = mm(pieces[:, rows], earlier)
            ahead = sums[0:groups] + sums[groups : 2 * groups] + sums[2 * groups : 3 * groups]
            total = ahead[:, block - 1 : block]
            level = jnp.where(behind_group, total - ahead + logs[:, rows], ahead)
            cum[p, :, rows] = level
            totals = jnp.where(lane == c, total, totals)
            whole = whole + total
            tails = spread(jnp.exp(total - level) * steps[:, rows], e, 2)
            xf = xs[p, rows, :].astype(F32)
            for o in range(2):
                weighted = (xf * tails[:, o * inner : (o + 1) * inner]).astype(BF)
                writer = coup[p, rows, 2 * o * state : (2 * o + 1) * state]
                contrib[p, o, c] = mm_tn(writer, weighted)
        left = row_of(whole)
        line = iota((msg.shape[2], TILE), 0)
        totals_sent = jnp.zeros((msg.shape[2], TILE), F32)
        for i in range(3):
            rounded = left.astype(BF).astype(F32)
            totals_sent = jnp.where(line == i, rounded, totals_sent)
            left = left - rounded
        totals_sent = totals_sent.astype(BF)
        fade[p] = spread(jnp.exp(totals), e, 3)[0:8]
        sums = [contrib[p, 0, 0], contrib[p, 1, count - 1]]
        for c in range(1, count):
            sums[0] = fade[p, c : c + 1, :inner] * sums[0] + contrib[p, 0, c]
            back = count - 1 - c
            sums[1] = fade[p, back : back + 1, inner:] * sums[1] + contrib[p, 1, back]
        for d in range(n):
            pieces = [v[d * part : (d + 1) * part] for v in sums]
            if 2 * part < 16:
                pieces.append(jnp.zeros((16 - 2 * part, inner), F32))
            msg[p, d, :, 0:inner] = jnp.concatenate(pieces, axis=0).astype(BF)
            msg[p, d, :, inner:] = totals_sent
        start_all(functools.partial(s_copy, p))
        got[p, pl.ds(me, 1)] = msg[p, pl.ds(me, 1)]

    def prepare_stacked(p):
        x = xs[p]
        first = p * 4 * state
        coup[p] = mm(x, coup_w_ref[:, first : first + 4 * state]).astype(BF)
        logits = mm_nt(step_w_ref[...], x) + step_b
        steps = jnp.maximum(logits, 0.0) + jnp.log1p(jnp.exp(-jnp.abs(logits)))
        logs = rates * steps
        step_t[p] = steps
        earlier = position(p, iota((block, block), 0)) <= position(p, iota((block, block), 1))
        earlier = jnp.where(earlier, 1.0, 0.0).astype(BF)

        def stack(v):
            return jnp.concatenate([v[:, rows_of(c)] for c in range(count)], axis=0)

        deep = count * groups
        behind_deep = lax.rem(iota((deep, 1), 0), 2 * heads) >= heads
        stacked = stack(logs)
        sums = mm(split(stacked, 3), earlier)
        ahead = sums[0:deep] + sums[deep : 2 * deep] + sums[2 * deep : 3 * deep]
        total = ahead[:, block - 1 : block]
        level = jnp.where(behind_deep, total - ahead + stacked, ahead)
        tail = jnp.exp(total - level) * stack(steps)
        e = spreader(p)
        lane = iota((groups, TILE), 1)
        totals = jnp.zeros((groups, TILE), F32)
        whole = jnp.zeros((groups, 1), F32)
        for c in range(count):
            rows = rows_of(c)
            these = slice(c * groups, (c + 1) * groups)
            cum[p, :, rows] = level[these]
            totals = jnp.where(lane == c, total[these], totals)
            whole = whole + total[these]
            tails = spread(tail[these], e, 2)
            xf = xs[p, rows, :].astype(F32)
            for o in range(2):
                weighted = (xf * tails[:, o * inner : (o + 1) * inner]).astype(BF)
                writer = coup[p, rows, 2 * o * state : (2 * o + 1) * state]
                contrib[p, o, c] = mm_tn(writer, weighted)
        left = row_of(whole)
        line = iota((msg.shape[2], TILE), 0)
        totals_sent = jnp.zeros((msg.shape[2], TILE), F32)
        for i in range(3):
            rounded = left.astype(BF).astype(F32)
            totals_sent = jnp.where(line == i, rounded, totals_sent)
            left = left - rounded
        totals_sent = totals_sent.astype(BF)
        fade[p] = spread(jnp.exp(totals), e, 3)[0:8]
        sums = [contrib[p, 0, 0], contrib[p, 1, count - 1]]
        for c in range(1, count):
            sums[0] = fade[p, c : c + 1, :inner] * sums[0] + contrib[p, 0, c]
            back = count - 1 - c
            sums[1] = fade[p, back : back + 1, inner:] * sums[1] + contrib[p, 1, back]
        for d in range(n):
            pieces = [v[d * part : (d + 1) * part] for v in sums]
            if 2 * part < 16:
                pieces.append(jnp.zeros((16 - 2 * part, inner), F32))
            msg[p, d, :, 0:inner] = jnp.concatenate(pieces, axis=0).astype(BF)
            msg[p, d, :, inner:] = totals_sent
        start_all(functools.partial(s_copy, p))
        got[p, pl.ds(me, 1)] = msg[p, pl.ds(me, 1)]

    def local(p):
        e = spreader(p)
        both_sides = e[:, :inner] + e[:, inner:]
        eyes = eye.astype(F32)
        rows_tile = min(block, TILE)
        even = jnp.bitwise_and(iota((1, 2 * head), 1), head) == 0
        for c in range(count):
            rows = rows_of(c)
            level = cum[p, :, rows]
            steps = step_t[p, :, rows]
            grown[p, rows, :] = spread(jnp.exp(level), e, 2)
            scaled = level * LOG2E
            source = scaled - jnp.log(steps) * LOG2E
            target = spread(scaled, eyes, 3)
            xf = xs[p, rows, :].astype(F32)
            pairs = []
            for j in range(heads // 2):
                lanes = xf[:, 2 * j * head : 2 * (j + 1) * head]
                pairs.append(
                    jnp.concatenate(
                        [jnp.where(even, lanes, 0.0), jnp.where(even, 0.0, lanes)], axis=0
                    ).astype(BF)
                )
            diagonals = [jnp.zeros((1, block), F32)] * 2
            for q in range(block // rows_tile):
                t0 = q * rows_tile
                mine = coup[p, c * block + t0 : c * block + t0 + rows_tile, :]
                ahead = mm_nt(mine[:, state : 2 * state], coup[p, rows, 0:state])
                behind = mm_nt(mine[:, 3 * state :], coup[p, rows, 2 * state : 3 * state])
                t = iota((rows_tile, block), 0) + t0
                s = iota((rows_tile, block), 1)
                after = position(p, t) > position(p, s)
                same = t == s
                scores = jnp.where(same, 0.0, jnp.where(after, ahead, behind))
                for o, v in enumerate((ahead, behind)):
                    found = jnp.sum(jnp.where(same, v, 0.0), axis=0, keepdims=True)
                    diagonals[o] = diagonals[o] + found

                def weights(h):
                    f = p * 2 * heads + h
                    g = f + heads
                    lead = target[t0 : t0 + rows_tile, f : f + 1] - source[f : f + 1, :]
                    back = target[t0 : t0 + rows_tile, g : g + 1] - source[g : g + 1, :]
                    return (scores * jnp.exp2(jnp.where(after, lead, back))).astype(BF)

                for j in range(heads // 2):
                    pair = jnp.concatenate([weights(2 * j), weights(2 * j + 1)], axis=1)
                    own[
                        p,
                        c * block + t0 : c * block + t0 + rows_tile,
                        2 * j * head : 2 * (j + 1) * head,
                    ] = mm(pair, pairs[j])
            diag = jnp.where(behind_group, diagonals[1], diagonals[0]) * steps
            diag = diag.astype(BF).astype(F32) + skips
            own[p, rows, :] += xf * spread(diag, both_sides, 2)

    def scan(p):
        wait_all(functools.partial(s_copy, p))
        e = spreader(p)
        logs = jnp.concatenate(
            [got[p, i, :, inner:].astype(F32)[0:8] for i in range(n)], axis=0
        )
        logs = logs + pltpu.roll(logs, 8 * n - 1, 0) + pltpu.roll(logs, 8 * n - 2, 0)
        pieces = split(jnp.exp(logs[:, 0:groups]), 3).reshape(3, 8 * n, groups)
        fades = sum(mm(pieces[i], e.astype(BF)) for i in range(3))
        entry = jnp.zeros((part, inner), F32)
        ahead = []
        for i in range(n):
            ahead.append(entry)
            entry = fades[8 * i : 8 * i + 1, :inner] * entry + got[p, i, :, 0:inner].astype(F32)[0:part]
        entry = jnp.zeros((part, inner), F32)
        for i in reversed(range(n)):
            pieces = [ahead[i], entry]
            if 2 * part < 16:
                pieces.append(jnp.zeros((16 - 2 * part, inner), F32))
            ent_out[p, i] = jnp.concatenate(pieces, axis=0).astype(BF)
            entry = (
                fades[8 * i : 8 * i + 1, inner:] * entry + got[p, i, :, 0:inner].astype(F32)[part : 2 * part]
            )
        start_all(functools.partial(e_copy, p))
        ent_in[p, pl.ds(me, 1)] = ent_out[p, pl.ds(me, 1)]

    def finish(p):
        wait_all(functools.partial(e_copy, p))
        arrived = [ent_in[p, i].astype(F32) for i in range(n)]
        entries = [[None] * count, [None] * count]
        for o in range(2):
            entry = jnp.concatenate([v[o * part : (o + 1) * part] for v in arrived], axis=0)
            order = range(count) if o == 0 else reversed(range(count))
            for c in order:
                entries[o][c] = entry.astype(BF)
                lanes = slice(o * inner, (o + 1) * inner)
                entry = fade[p, c : c + 1, lanes] * entry + contrib[p, o, c]
        for c in range(count):
            rows = rows_of(c)
            result = own[p, rows, :]
            for o in range(2):
                reader = coup[p, rows, (2 * o + 1) * state : (2 * o + 2) * state]
                carried = mm(reader, entries[o][c])
                result = result + carried * grown[p, rows, o * inner : (o + 1) * inner]
            if p == 0:
                own[p, rows, :] = result
            else:
                result = result.astype(BF)
                for i in range(n):
                    col_out[i, c * span : (c + 1) * span, :] = result[i * span : (i + 1) * span]

    prepare(1)
    @pl.when(me < n - 1)
    def _():
        halo_copy(1, me + 1).wait_recv()
        halo_copy(0, me + 1).wait_send()

    @pl.when(me == n - 1)
    def _():
        halo[1] = jnp.zeros((width, tokens), BF)

    @pl.when(me > 0)
    def _():
        halo_copy(0, me - 1).wait_recv()
        halo_copy(1, me - 1).wait_send()

    @pl.when(me == 0)
    def _():
        halo[0] = jnp.zeros((width, tokens), BF)

    for slot, a in ((0, 0), (1, 2)):
        rim = mm_tn(normed(halo[slot].astype(F32)), in_w_ref[:, :inner]).astype(BF)
        pre[a, 8 : tokens + 8, :] = rim.astype(F32)
    for c in range(tokens // TILE):
        span_rows = slice(c * TILE, (c + 1) * TILE + 16)
        done = depthwise(lambda a, lanes: pre[a, span_rows, lanes], conv_w_ref, conv_b, TILE)
        xs[0, c * TILE : (c + 1) * TILE, :] = done.astype(BF)
    prepare_stacked(0)
    scan(1)
    local(1)
    scan(0)
    finish(1)
    start_all(c_copy)
    col_in[pl.ds(me, 1)] = col_out[pl.ds(me, 1)]
    local(0)
    finish(0)
    wait_sent(r_copy)
    for p in range(2):
        wait_sent(functools.partial(s_copy, p))
        wait_sent(functools.partial(e_copy, p))
    wait_all(c_copy)
    wait_sent(c_copy)
    for c in range(tokens // TILE):
        rows = slice(c * TILE, (c + 1) * TILE)
        per = TILE // band
        col = col_in[c * per : (c + 1) * per].astype(F32).reshape(TILE, inner)
        gated = (own[0, rows, :] + col) * gate[rows, :]
        mean_square = jnp.mean(gated * gated, axis=-1, keepdims=True)
        normy = (gated * lax.rsqrt(mean_square + EPSILON) * out_gain).astype(BF)
        out_ref[0, :, rows] = (
            region_ref[:, rows].astype(F32) + mm_nt(out_w_ref[...], normy)
        ).astype(BF)


def body(n, *args):
    region = args[0]
    _, tokens, width = region.shape
    inner = args[11].shape[0]
    groups = args[7].shape[0]
    heads = groups // 4
    state = args[5].shape[1] // 8
    band = tokens // n
    part = state // n
    block = max(TILE, 16 * n)
    count = tokens // block
    fold = TILE // band
    cell_rows = (width // fold + 8 + 15) // 16 * 16
    flat = [v if v.ndim > 1 else v.reshape(1, -1) for v in args]
    for i in (4, 10):
        if args[i].shape[0] % TILE == 0:
            flat[i] = args[i].reshape(-1, TILE)
    flat[0] = jnp.swapaxes(region, 1, 2)
    flat[6] = flat[6].T
    flat[11] = flat[11].T
    ent_rows = max(16, 2 * part)
    dma = pltpu.SemaphoreType.DMA
    vmem = pltpu.VMEM
    flat = [pltpu.with_memory_space_constraint(v, pltpu.HBM) for v in flat]
    out = pl.pallas_call(
        functools.partial(kernel, n, heads, state, block),
        out_shape=jax.ShapeDtypeStruct(flat[0].shape, BF),
        in_specs=[pl.BlockSpec(memory_space=pltpu.HBM)] * len(flat),
        out_specs=pl.BlockSpec(memory_space=pltpu.VMEM),
        scratch_shapes=[
            vmem((width, tokens), BF),
            *[vmem(v.shape, v.dtype) for v in flat[1:]],
            vmem((n, cell_rows, TILE), BF),
            vmem((n, cell_rows, TILE), BF),
            vmem((2, width, tokens), BF),
            vmem((3, tokens + 16, inner), F32),
            vmem((n + 2, band + 16, inner), F32),
            vmem((tokens, inner), F32),
            vmem((2, tokens, inner), BF),
            vmem((2, tokens, 4 * state), BF),
            vmem((2, groups, tokens), F32),
            vmem((2, groups, tokens), F32),
            vmem((2, 2, count, state, inner), F32),
            vmem((2, 8, 2 * inner), F32),
            vmem((2, tokens, 2 * inner), F32),
            vmem((2, tokens, inner), F32),
            vmem((2, n, ent_rows, inner + TILE), BF),
            vmem((2, n, ent_rows, inner + TILE), BF),
            vmem((2, n, ent_rows, inner), BF),
            vmem((2, n, ent_rows, inner), BF),
            vmem((n, band, inner), BF),
            vmem((n, band, inner), BF),
            dma((len(flat),)),
            dma((n,)),
            dma((n,)),
            dma((2,)),
            dma((2,)),
            dma((2, n)),
            dma((2, n)),
            dma((2, n)),
            dma((2, n)),
            dma((n,)),
            dma((n,)),
        ],
        compiler_params=pltpu.CompilerParams(
            collective_id=0, has_side_effects=True, vmem_limit_bytes=40 * 1024 * 1024
        ),
    )(*flat)
    return jnp.swapaxes(out, 1, 2)


def solution(mesh):
    in_specs = (P(("dp", "seq"), None, None),) + (P(),) * 11
    return jax.shard_map(
        functools.partial(body, mesh.shape["seq"]),
        mesh=mesh,
        in_specs=in_specs,
        out_specs=P(("dp", "seq"), None, None),
        check_vma=False,
    )
```
